128 devices in a mesh: section: 8 (over x, core), tensor: 16 (over z, y).
Axes of the slice: x: 4, y: 4, z: 4, core: 2. Of those that a mesh axis runs over, the one named last changes fastest.
Arguments:
- token_ids: int32 [4, 32], replicated, may hold values from 0 to 511
- block_types: int32 [8], P('section'), may hold values from 0 to 1
- embed_table: bfloat16 [512, 8192], P('section'), may hold values from -6 to 6
- proj_weights: bfloat16 [8, 8192, 4096], P('section', None, 'tensor'), may hold values from -0.0625 to 0.0625
- norm_gains: float32 [8, 8192], P('section'), may hold values from 0.25 to 1.75
- conv_filters: bfloat16 [8, 128, 4096], P('section', None, 'tensor'), may hold values from -0.59765625 to 0.59765625
- conv_caches: bfloat16 [8, 32, 127, 4096], P('section', None, None, 'tensor'), may hold values from -6 to 6
- final_gain: float32 [8192], replicated, may hold values from 0.25 to 1.75
- unembed: bfloat16 [8192, 512], P(None, 'section'), may hold values from -0.1875 to 0.1875
Outputs:
- logits: float32 [4, 32, 512], P(None, None, 'section')
The draws below stay inside these ranges and needn't reach their ends.
All inputs are finite; a program needn't handle non-finite values.
Results may differ from the reference program's by a relative error of at most 0.02.
Values may be sent and summed in bfloat16 or wider, within the bound.
No kernel may reach another device: no remote copies, remote signals or barrier semaphores. Data moves between devices by JAX's collectives and lax.ppermute only.
A program may use at most 64 MiB of HBM per device.

```python
import jax
import jax.numpy as jnp
from jax import lax

D = 8192
VOCAB = 512
CH = 4096
TAPS = 128
SHORT = 7
STEPS = 4
REQ = 32
N_SECTION = 8
N_TENSOR = 16


def with_ends(entries, stream_key, least, largest):
    place = [jax.random.randint(jax.random.fold_in(stream_key, axis), (), 0, length) for axis, length in enumerate(entries.shape)]
    widest = entries.shape.index(max(entries.shape))
    neighbour = place[:widest] + [(place[widest] + 1) % entries.shape[widest]] + place[widest + 1:]
    return entries.at[tuple(place)].set(least).at[tuple(neighbour)].set(largest)


def steps_of(stream_key, shape, shards, least, high):
    loudness, own = 1.0, jax.random.fold_in(stream_key, 6)
    for position, parts in shards:
        draws = jnp.exp(jax.random.uniform(jax.random.fold_in(own, position), (parts,), jnp.float32, least / len(shards), high / len(shards)))
        loudness = loudness * jnp.repeat(draws, shape[position] // parts).reshape([-1 if axis == position else 1 for axis in range(len(shape))])
    return loudness


def noise(rng, shape, width, limit, split=(), held_as=jnp.bfloat16):
    array = width * jax.random.normal(rng, shape, jnp.float32)
    if split:
        array = array * steps_of(rng, shape, split, -0.22, 0.18)
    return jnp.clip(array, -limit, limit).astype(held_as)


def setup_inputs(seed: int = 0) -> dict:
    key_of = jax.random.split(jax.random.key(seed), 10)
    return {
        "token_ids": with_ends(jax.random.randint(key_of[0], (STEPS, REQ), 0, VOCAB), jax.random.fold_in(key_of[0], 1), 0, VOCAB - 1).astype(jnp.int32),
        "block_types": with_ends(jax.random.randint(key_of[1], (N_SECTION,), 0, 2), jax.random.fold_in(key_of[1], 1), 0, 1).astype(jnp.int32),
        "embed_table": noise(key_of[2], (VOCAB, D), 1.0, 6.0, ((0, 8),)),
        "proj_weights": noise(key_of[3], (N_SECTION, D, CH), D ** -0.5, 0.0625, ((0, 8), (2, 16))),
        "norm_gains": jnp.clip(1.0 + 0.15 * jax.random.normal(key_of[4], (N_SECTION, D), jnp.float32), 0.25, 1.75),
        "conv_filters": noise(key_of[5], (N_SECTION, TAPS, CH), 0.1, 0.59765625, ((0, 8), (2, 16))),
        "conv_caches": noise(key_of[6], (N_SECTION, REQ, TAPS - 1, CH), 1.0, 6.0, ((0, 8), (3, 16))),
        "final_gain": jnp.clip(1.0 + 0.15 * jax.random.normal(key_of[7], (D,), jnp.float32), 0.25, 1.75),
        "unembed": noise(key_of[8], (D, VOCAB), (D // 9) ** -0.5, 0.1875, ((1, 8),)),
    }


def rms_scale(values, scale_row):
    values = values.astype(jnp.float32)
    mean_square = lax.optimization_barrier(jnp.mean(values * values, axis=-1, keepdims=True))
    return values * lax.rsqrt(mean_square + 1e-06) * scale_row

def causal_conv(signal, tap_rows, block_kind, history):
    tap_mask = jnp.where(block_kind == 1, 1.0, (jnp.arange(TAPS) < SHORT).astype(jnp.float32))
    weights = tap_rows.astype(jnp.float32) * tap_mask[:, None]
    flipped = weights[::-1]
    series = jnp.concatenate([history.astype(jnp.float32), jnp.transpose(signal, (1, 0, 2)).astype(jnp.float32)], axis=1)
    results = []
    for moment in range(STEPS):
        window = series[:, moment:moment + TAPS]
        results.append(jnp.einsum('ric,ic->rc', window, flipped, precision=lax.Precision.HIGHEST))
    return jnp.stack(results)

def reference(token_ids, block_types, embed_table, proj_weights, norm_gains, conv_filters, conv_caches, final_gain, unembed):
    residual = jnp.take(embed_table, token_ids, axis=0)
    width_part = CH // N_TENSOR
    carried = None
    for layer_section in range(N_SECTION):
        weight = proj_weights[layer_section]
        block_kind = block_types[layer_section]
        if layer_section % 2 == 0:
            normed = rms_scale(residual, norm_gains[layer_section]).astype(jnp.bfloat16)
            projected = jnp.dot(normed, weight, preferred_element_type=jnp.float32).astype(jnp.bfloat16)
            carried = causal_conv(projected, conv_filters[layer_section], block_kind, conv_caches[layer_section]).astype(jnp.bfloat16)
        else:
            mixed_rows = causal_conv(carried, conv_filters[layer_section], block_kind, conv_caches[layer_section])
            gated_rows = (carried.astype(jnp.float32) * mixed_rows).astype(jnp.bfloat16)
            summed = jnp.zeros(residual.shape, jnp.float32)
            for group_index in range(N_TENSOR):
                start_col = group_index * width_part
                partial_value = jnp.dot(gated_rows[..., start_col:start_col + width_part], weight[:, start_col:start_col + width_part].T, preferred_element_type=jnp.float32).astype(jnp.bfloat16)
                partial_value = lax.optimization_barrier(partial_value)
                summed = summed + partial_value.astype(jnp.float32)
            residual = (residual.astype(jnp.float32) + norm_gains[layer_section] * summed).astype(jnp.bfloat16)
    normed = rms_scale(residual, final_gain).astype(jnp.bfloat16)
    return jnp.dot(normed, unembed, preferred_element_type=jnp.float32)
```

```python
import jax
import jax.numpy as jnp
from jax import lax
from jax.sharding import PartitionSpec as P

SHORT = 7
CORES = 2


def swap_cores(block):
    devices = range(lax.axis_size("section"))
    return lax.ppermute(block, "section", [(i, i ^ 1) for i in devices])


def to_plane(block, source, target):
    route = [(CORES * source + core, CORES * target + core) for core in range(CORES)]
    return lax.ppermute(block, "section", route)


def exchange(blocks):
    return lax.all_to_all(blocks, "tensor", 0, 0)


def gather(block):
    return exchange(jnp.broadcast_to(block, (lax.axis_size("tensor"),) + block.shape))


def on_device(
    token_ids,
    block_types,
    embed_table,
    proj_weights,
    norm_gains,
    conv_filters,
    conv_caches,
    final_gain,
    unembed,
):
    f32, bf16 = jnp.float32, jnp.bfloat16
    planes = lax.axis_size("section") // CORES
    section = lax.axis_index("section")
    plane, core = section // CORES, section % CORES
    groups = lax.axis_size("tensor")
    group = lax.axis_index("tensor")
    steps, requests = token_ids.shape
    own = requests // CORES
    rows = steps * own
    vocab_local, width = embed_table.shape
    part = width // groups
    chan = proj_weights.shape[2]
    taps = conv_filters.shape[1]

    def pair(mine):
        other = swap_cores(mine)
        even = jnp.where(core == 0, mine, other)
        odd = jnp.where(core == 0, other, mine)
        return even, odd

    ids = token_ids.reshape(steps, CORES, own).transpose(1, 0, 2).reshape(CORES, rows)
    vocab_ids = section * vocab_local + jnp.arange(vocab_local, dtype=jnp.int32)
    one_hot = (ids[:, :, None] == vocab_ids).astype(bf16)
    table_part = lax.dynamic_slice_in_dim(embed_table, group * part, part, 1)
    found = jnp.einsum("crv,vd->crd", one_hot, table_part, preferred_element_type=f32).astype(bf16)
    kept = lax.dynamic_index_in_dim(found, core, 0, keepdims=False)
    given = lax.dynamic_index_in_dim(found, 1 - core, 0, keepdims=False)
    on_chip = kept + swap_cores(given)
    chunk = on_chip
    for source in range(1, planes):
        chunk = chunk + to_plane(on_chip, source, 0)

    weight_in, weight_out = pair(proj_weights[0])
    gain_in, gain_out = pair(norm_gains[0])
    weight_in = weight_in.reshape(groups, part, chan)
    weight_out = weight_out.reshape(groups, part, chan)
    gain_in = gain_in.reshape(groups, 1, part)
    gain_out = lax.dynamic_slice_in_dim(gain_out, group * part, part, 0)

    mask = jnp.where(block_types[0] == 1, 1.0, (jnp.arange(taps) < SHORT).astype(f32))
    filt = (conv_filters[0].astype(f32) * mask[:, None]).astype(bf16)
    flipped = filt[::-1]
    history = conv_caches[0]
    length = history.shape[1]
    shifted = jnp.stack(
        [
            jnp.concatenate([jnp.zeros((k, chan), bf16), flipped[: length - k]], 0)
            for k in range(steps)
        ]
    )
    terms = jnp.einsum("krc,brc->kbc", shifted, history, preferred_element_type=f32)
    terms = terms.reshape(steps, CORES, own, chan).transpose(1, 0, 2, 3)
    terms_kept = lax.dynamic_index_in_dim(terms, core, 0, keepdims=False)
    terms_given = lax.dynamic_index_in_dim(terms, 1 - core, 0, keepdims=False)
    terms_other = swap_cores(terms_given)
    base_in = jnp.where(core == 0, terms_kept, terms_other)
    base_out = jnp.where(core == 0, terms_other, terms_kept)
    lags_in, lags_out = pair(filt[:steps].astype(f32))

    def convolve(signal, base, lags):
        signal = signal.astype(f32).reshape(steps, own, chan)
        results = []
        for k in range(steps):
            total = base[k]
            for lag in range(k + 1):
                total = total + lags[lag] * signal[k - lag]
            results.append(total)
        return jnp.stack(results).reshape(rows, chan)

    for layer in range(planes):
        full = gather(chunk).astype(f32)
        mean_square = jnp.sum(full * full, axis=(0, 2), keepdims=True) / width
        normed = (full * lax.rsqrt(mean_square + 1e-06) * gain_in).astype(bf16)
        a = jnp.einsum("trk,tkc->rc", normed, weight_in, preferred_element_type=f32).astype(bf16)
        z = convolve(a, base_in, lags_in).astype(bf16)
        g = (z.astype(f32) * convolve(z, base_out, lags_out)).astype(bf16)
        partial = jnp.einsum("rc,tkc->trk", g, weight_out, preferred_element_type=f32)
        summed = jnp.sum(exchange(partial.astype(bf16)).astype(f32), axis=0)
        chunk = (chunk.astype(f32) + gain_out * summed).astype(bf16)
        if layer < planes - 1:
            chunk = to_plane(chunk, layer, layer + 1)

    last = planes - 1
    shared = jnp.where(plane == last, chunk, jnp.zeros_like(chunk))
    for target in range(last):
        shared = shared + to_plane(chunk, last, target)
    other = swap_cores(shared)
    both = jnp.where(core == 0, jnp.stack([shared, other]), jnp.stack([other, shared]))
    both = both.reshape(CORES * rows, part).astype(f32)
    gain_part = lax.dynamic_slice_in_dim(final_gain, group * part, part, 0)
    head_part = lax.dynamic_slice_in_dim(unembed, group * part, part, 0)
    squares = jnp.sum(both * both, axis=1, keepdims=True)
    scores = jnp.dot((both * gain_part).astype(bf16), head_part, preferred_element_type=f32)
    packed = jnp.concatenate([scores, squares], 1)
    totals = jnp.sum(gather(packed), axis=0)
    cols = unembed.shape[1]
    logits = totals[:, :cols] * lax.rsqrt(totals[:, cols:] / width + 1e-06)
    return logits.reshape(CORES, steps, own, cols).transpose(1, 0, 2, 3).reshape(steps, requests, cols)


def solution(mesh):
    placed = (
        P(),
        P("section"),
        P("section", None),
        P("section", None, "tensor"),
        P("section", None),
        P("section", None, "tensor"),
        P("section", None, None, "tensor"),
        P(),
        P(None, "section"),
    )
    return jax.shard_map(
        on_device, mesh=mesh, in_specs=placed, out_specs=P(None, None, "section"), check_vma=False
    )
```

```python
import jax
import jax.numpy as jnp
from jax import lax
from jax.experimental import pallas as pl
from jax.experimental.pallas import tpu as pltpu
from jax.sharding import PartitionSpec as P

SHORT = 7
CORES = 2
RECUT = 2
LEAD = 8
EXTRA = 8


def swap_cores(block):
    devices = range(lax.axis_size("section"))
    return lax.ppermute(block, "section", [(i, i ^ 1) for i in devices])


def to_plane(block, source, target):
    route = [(CORES * source + core, CORES * target + core) for core in range(CORES)]
    return lax.ppermute(block, "section", route)


def exchange(blocks):
    return lax.all_to_all(blocks, "tensor", 0, 0)


def copies(block):
    return jnp.broadcast_to(block, (lax.axis_size("tensor"),) + block.shape)


def unset(like):
    return pl.pallas_call(
        lambda out: None,
        out_shape=jax.ShapeDtypeStruct(like.shape, like.dtype),
        out_specs=pl.BlockSpec(memory_space=pl.ANY),
    )()


def terms_kernel(filt_ref, history_ref, out_ref, shifted):
    steps = out_ref.shape[0]
    length = history_ref.shape[1]
    for k in range(steps):
        shifted[k] = filt_ref[LEAD - k : LEAD - k + length, :]

    def one_request(b, carry):
        rows = history_ref[b].astype(jnp.float32)
        for k in range(steps):
            out_ref[k, pl.ds(b, 1), :] = jnp.sum(shifted[k] * rows, axis=0, keepdims=True)
        return carry

    lax.fori_loop(0, history_ref.shape[0], one_request, 0)


def cache_terms(filt, history, steps):
    requests, length, chan = history.shape
    padded = jnp.pad(filt[::-1].astype(jnp.float32), ((LEAD, 0), (0, 0)))
    return pl.pallas_call(
        terms_kernel,
        out_shape=jax.ShapeDtypeStruct((steps, requests, chan), jnp.float32),
        in_specs=[pl.BlockSpec(memory_space=pltpu.VMEM)] * 2,
        out_specs=pl.BlockSpec(memory_space=pltpu.VMEM),
        scratch_shapes=[pltpu.VMEM((steps, length, chan), jnp.float32)],
        compiler_params=pltpu.CompilerParams(vmem_limit_bytes=24 << 20),
        cost_estimate=pl.CostEstimate(
            flops=2 * steps * requests * length * chan,
            bytes_accessed=2 * requests * length * chan,
            transcendentals=0,
        ),
    )(padded, history)


def as_row_pair(column, width):
    row = jnp.pad(column.reshape(1, -1), ((0, 0), (0, width - column.shape[0])))
    high = row.astype(jnp.bfloat16)
    low = (row - high.astype(jnp.float32)).astype(jnp.bfloat16)
    return jnp.pad(jnp.concatenate([high, low], 0), ((0, EXTRA - 2), (0, 0)))


def on_device(
    token_ids,
    block_types,
    embed_table,
    proj_weights,
    norm_gains,
    conv_filters,
    conv_caches,
    final_gain,
    unembed,
):
    f32, bf16 = jnp.float32, jnp.bfloat16
    planes = lax.axis_size("section") // CORES
    section = lax.axis_index("section")
    plane, core = section // CORES, section % CORES
    groups = lax.axis_size("tensor")
    group = lax.axis_index("tensor")
    steps, requests = token_ids.shape
    own = requests // CORES
    rows = steps * own
    vocab_local, width = embed_table.shape
    part = width // groups
    chan = proj_weights.shape[2]
    taps = conv_filters.shape[1]
    cols = unembed.shape[1]

    ids = token_ids.reshape(steps, CORES, own).transpose(1, 0, 2).reshape(CORES, rows)
    vocab_ids = section * vocab_local + jnp.arange(vocab_local, dtype=jnp.int32)
    table_part = lax.dynamic_slice_in_dim(embed_table, group * part, part, 1)

    def find(half):
        half_ids = lax.dynamic_index_in_dim(ids, half, 0, keepdims=False)
        one_hot = (half_ids[:, None] == vocab_ids).astype(bf16)
        return jnp.dot(one_hot, table_part, preferred_element_type=f32).astype(bf16)

    on_chip = find(core) + swap_cores(find(1 - core))
    on_chip, mine, small = lax.optimization_barrier(
        (on_chip, proj_weights[0], (norm_gains[0], unembed))
    )
    my_gain, unembed = small

    def pair(mine):
        other = swap_cores(mine)
        even = jnp.where(core == 0, mine, other)
        odd = jnp.where(core == 0, other, mine)
        return even, odd

    chunk = on_chip
    for source in range(1, planes):
        chunk = chunk + to_plane(on_chip, source, 0)
    blocks, filters, history = lax.optimization_barrier(
        (copies(chunk), conv_filters[0], conv_caches[0])
    )
    gathered = exchange(blocks)

    mask = jnp.where(block_types[0] == 1, 1.0, (jnp.arange(taps) < SHORT).astype(f32))
    filt = filters.astype(f32) * mask[:, None]
    terms = cache_terms(filt, history, steps).reshape(steps, CORES, own, chan)
    terms_kept = lax.dynamic_index_in_dim(terms, core, 1, keepdims=False)
    terms_given = lax.dynamic_index_in_dim(terms, 1 - core, 1, keepdims=False)
    terms_other = swap_cores(terms_given)
    base_in = jnp.where(core == 0, terms_kept, terms_other)
    base_out = jnp.where(core == 0, terms_other, terms_kept)
    lags_in, lags_out = pair(filt[:steps])
    weight_in, weight_out = pair(mine.reshape(groups, part, chan))
    gain_in, gain_out = pair(my_gain)
    gain_in_all = gain_in.reshape(groups, 1, part)
    gain_in = lax.dynamic_slice_in_dim(gain_in, group * part, part, 0)
    gain_out = lax.dynamic_slice_in_dim(gain_out, group * part, part, 0)
    head = pair(lax.dynamic_slice_in_dim(unembed, group * part, part, 0))
    head = jnp.concatenate(head, 1)
    head_gain = lax.dynamic_slice_in_dim(final_gain, group * part, part, 0)

    def convolve(signal, base, lags):
        signal = signal.astype(f32).reshape(steps, own, chan)
        results = []
        for k in range(steps):
            total = base[k]
            for lag in range(k + 1):
                total = total + lags[lag] * signal[k - lag]
            results.append(total)
        return jnp.stack(results).reshape(rows, chan)

    def gate(a):
        z = convolve(a.astype(bf16), base_in, lags_in).astype(bf16)
        return (z.astype(f32) * convolve(z, base_out, lags_out)).astype(bf16)

    def native(chunk, gathered):
        full = gathered.astype(f32)
        mean_square = jnp.sum(full * full, axis=(0, 2), keepdims=True) / width
        normed = (full * lax.rsqrt(mean_square + 1e-06) * gain_in_all).astype(bf16)
        g = gate(jnp.einsum("trk,tkc->rc", normed, weight_in, preferred_element_type=f32))
        partial = jnp.einsum("rc,tkc->trk", g, weight_out, preferred_element_type=f32)
        summed = jnp.sum(exchange(partial.astype(bf16)).astype(f32), axis=0)
        return (chunk.astype(f32) + gain_out * summed).astype(bf16)

    def recut(chunk, cut_in, cut_out):
        values = chunk.astype(f32)
        squares = jnp.sum(values * values, axis=1, keepdims=True)
        scaled = (values * gain_in).astype(bf16)
        partial = jnp.einsum("rk,tkc->trc", scaled, cut_in, preferred_element_type=f32)
        packed = jnp.concatenate([partial.astype(bf16), copies(as_row_pair(squares, chan))], 1)
        totals = jnp.sum(exchange(packed).astype(f32), axis=0)
        square = (totals[rows] + totals[rows + 1])[:rows, None]
        g = gate(totals[:rows] * lax.rsqrt(square / width + 1e-06))
        whole = exchange(copies(g))
        summed = jnp.einsum("trc,tkc->rk", whole, cut_out, preferred_element_type=f32)
        return (values + gain_out * summed).astype(bf16)

    def cut(mine):
        return pair(exchange(mine))

    cut_in, cut_out = lax.cond(
        plane >= RECUT,
        cut,
        lambda mine: (unset(mine), unset(mine)),
        mine.reshape(groups, part, chan),
    )
    chunk = lax.cond(plane == 0, native, lambda chunk, gathered: chunk, chunk, gathered)
    for layer in range(1, planes):
        chunk = to_plane(chunk, layer - 1, layer)
        if layer < RECUT:
            chunk = lax.cond(
                plane == layer, lambda c: native(c, exchange(copies(c))), lambda c: c, chunk
            )
            if layer == RECUT - 1:
                chunk, cut_in, cut_out = lax.optimization_barrier((chunk, cut_in, cut_out))
        else:
            chunk = lax.cond(
                plane == layer, recut, lambda c, cut_in, cut_out: c, chunk, cut_in, cut_out
            )

    last = planes - 1
    shared = jnp.where(plane == last, chunk, jnp.zeros_like(chunk))
    for target in range(last):
        shared = shared + to_plane(chunk, last, target)
    shared = shared.astype(f32)
    squares = jnp.sum(shared * shared, axis=1, keepdims=True)
    scores = jnp.dot((shared * head_gain).astype(bf16), head, preferred_element_type=f32)
    packed = jnp.concatenate([scores.astype(bf16), as_row_pair(squares, CORES * cols)], 0)
    totals = jnp.sum(exchange(copies(packed)).astype(f32), axis=0)
    square = (totals[rows] + totals[rows + 1])[:rows, None]
    logits = totals[:rows] * lax.rsqrt(square / width + 1e-06)
    kept = jnp.where(core == 0, logits[:, :cols], logits[:, cols:])
    other = swap_cores(jnp.where(core == 0, logits[:, cols:], logits[:, :cols]))
    both = jnp.where(core == 0, jnp.stack([kept, other]), jnp.stack([other, kept]))
    return both.reshape(CORES, steps, own, cols).transpose(1, 0, 2, 3).reshape(steps, requests, cols)


def solution(mesh):
    placed = (
        P(),
        P("section"),
        P("section", None),
        P("section", None, "tensor"),
        P("section", None),
        P("section", None, "tensor"),
        P("section", None, None, "tensor"),
        P(),
        P(None, "section"),
    )
    return jax.shard_map(
        on_device, mesh=mesh, in_specs=placed, out_specs=P(None, None, "section"), check_vma=False
    )
```

```python
import jax
import jax.numpy as jnp
from jax import lax
from jax.experimental import pallas as pl
from jax.experimental.pallas import tpu as pltpu
from jax.sharding import PartitionSpec as P

SHORT = 7
CORES = 2
LEAD = 8
EXTRA = 8


def swap_cores(block):
    devices = range(lax.axis_size("section"))
    return lax.ppermute(block, "section", [(i, i ^ 1) for i in devices])


def to_plane(block, source, target):
    route = [(CORES * source + core, CORES * target + core) for core in range(CORES)]
    return lax.ppermute(block, "section", route)


def exchange(blocks):
    return lax.all_to_all(blocks, "tensor", 0, 0)


def copies(block):
    return jnp.broadcast_to(block, (lax.axis_size("tensor"),) + block.shape)


def unset(like):
    return pl.pallas_call(
        lambda out: None,
        out_shape=jax.ShapeDtypeStruct(like.shape, like.dtype),
        out_specs=pl.BlockSpec(memory_space=pl.ANY),
    )()


def terms_kernel(filt_ref, history_ref, out_ref, shifted):
    steps = out_ref.shape[0]
    length = history_ref.shape[1]

    @pl.when(pl.program_id(0) == 0)
    def _():
        for k in range(steps):
            shifted[k] = filt_ref[LEAD - k : LEAD - k + length, :]

    def one_request(b, carry):
        rows = history_ref[b].astype(jnp.float32)
        for k in range(steps):
            out_ref[k, pl.ds(b, 1), :] = jnp.sum(shifted[k] * rows, axis=0, keepdims=True)
        return carry

    lax.fori_loop(0, history_ref.shape[0], one_request, 0)


def cache_terms(filt, history, steps):
    requests, length, chan = history.shape
    padded = jnp.pad(filt[::-1].astype(jnp.float32), ((LEAD, 0), (0, 0)))
    block = LEAD
    return pl.pallas_call(
        terms_kernel,
        grid=(requests // block,),
        out_shape=jax.ShapeDtypeStruct((steps, requests, chan), jnp.float32),
        in_specs=[
            pl.BlockSpec(padded.shape, lambda i: (0, 0)),
            pl.BlockSpec((block, length, chan), lambda i: (i, 0, 0)),
        ],
        out_specs=pl.BlockSpec((steps, block, chan), lambda i: (0, i, 0)),
        scratch_shapes=[pltpu.VMEM((steps, length, chan), jnp.float32)],
        compiler_params=pltpu.CompilerParams(vmem_limit_bytes=24 << 20),
        cost_estimate=pl.CostEstimate(
            flops=2 * steps * requests * length * chan,
            bytes_accessed=2 * requests * length * chan,
            transcendentals=0,
        ),
    )(padded, history)


def fetch_kernel(choice_ref, *refs):
    count = (len(refs) - 2) // 2
    sources, out_ref, sem = refs[: 2 * count], refs[-2], refs[-1]
    depth = out_ref.shape[1] // count
    for pick in range(2):

        @pl.when(choice_ref[0] == pick)
        def _():
            moves = [
                pltpu.make_async_copy(
                    sources[pick * count + n], out_ref.at[:, pl.ds(n * depth, depth)], sem.at[n]
                )
                for n in range(count)
            ]
            for move in moves:
                move.start()
            for move in moves:
                move.wait()


def fetch(choice, first, second):
    count = len(first)
    groups, depth, chan = first[0].shape
    size = groups * depth * count * chan
    return pl.pallas_call(
        fetch_kernel,
        out_shape=jax.ShapeDtypeStruct((groups, depth * count, chan), first[0].dtype),
        in_specs=[pl.BlockSpec(memory_space=pltpu.SMEM)]
        + [pl.BlockSpec(memory_space=pl.ANY)] * (2 * count),
        out_specs=pl.BlockSpec(memory_space=pltpu.VMEM),
        scratch_shapes=[pltpu.SemaphoreType.DMA((count,))],
        compiler_params=pltpu.CompilerParams(vmem_limit_bytes=24 << 20),
        cost_estimate=pl.CostEstimate(flops=0, bytes_accessed=4 * size, transcendentals=0),
    )(choice.reshape(1), *first, *second)


def as_row_pair(column, width):
    row = jnp.pad(column.reshape(1, -1), ((0, 0), (0, width - column.shape[0])))
    high = row.astype(jnp.bfloat16)
    low = (row - high.astype(jnp.float32)).astype(jnp.bfloat16)
    return jnp.pad(jnp.concatenate([high, low], 0), ((0, EXTRA - 2), (0, 0)))


def on_device(
    token_ids,
    block_types,
    embed_table,
    proj_weights,
    norm_gains,
    conv_filters,
    conv_caches,
    final_gain,
    unembed,
):
    f32, bf16 = jnp.float32, jnp.bfloat16
    planes = lax.axis_size("section") // CORES
    section = lax.axis_index("section")
    plane, core = section // CORES, section % CORES
    groups = lax.axis_size("tensor")
    group = lax.axis_index("tensor")
    steps, requests = token_ids.shape
    own = requests // CORES
    rows = steps * own
    vocab_local, width = embed_table.shape
    part = width // groups
    chan = proj_weights.shape[2]
    taps = conv_filters.shape[1]
    cols = unembed.shape[1]

    vocab_ids = section * vocab_local + jnp.arange(vocab_local, dtype=jnp.int32)
    table_part = lax.dynamic_slice_in_dim(embed_table, group * part, part, 1)

    def find(half):
        ids = lax.dynamic_slice_in_dim(token_ids, half * own, own, 1)
        one_hot = (ids[:, :, None] == vocab_ids).astype(bf16).reshape(rows, vocab_local)
        return jnp.dot(one_hot, table_part, preferred_element_type=f32).astype(bf16)

    on_chip = find(core) + swap_cores(find(1 - core))
    on_chip, mine, small = lax.optimization_barrier(
        (on_chip, proj_weights[0].reshape(groups, part, chan), (norm_gains[0], unembed))
    )
    my_gain, unembed = small

    def pair(mine):
        other = swap_cores(mine)
        even = jnp.where(core == 0, mine, other)
        odd = jnp.where(core == 0, other, mine)
        return even, odd

    chunk = on_chip
    for source in range(1, planes):
        chunk = chunk + to_plane(on_chip, source, 0)
    gain_in, gain_out = pair(my_gain)
    gain_in_all = gain_in.reshape(groups, 1, part)
    gain_in = lax.dynamic_slice_in_dim(gain_in, group * part, part, 0)
    gain_out = lax.dynamic_slice_in_dim(gain_out, group * part, part, 0)

    def setup(filters, history):
        mask = jnp.where(block_types[0] == 1, 1.0, (jnp.arange(taps) < SHORT).astype(f32))
        filt = filters.astype(f32) * mask[:, None]
        terms = cache_terms(filt, history, steps).reshape(steps, CORES, own, chan)
        terms_kept = lax.dynamic_index_in_dim(terms, core, 1, keepdims=False)
        terms_given = lax.dynamic_index_in_dim(terms, 1 - core, 1, keepdims=False)
        terms_other = swap_cores(terms_given)
        base_in = jnp.where(core == 0, terms_kept, terms_other)
        base_out = jnp.where(core == 0, terms_other, terms_kept)
        lags_in, lags_out = pair(filt[:steps])
        return base_in, lags_in, base_out, lags_out

    def convolve(signal, base, lags):
        signal = signal.astype(f32).reshape(steps, own, chan)
        results = []
        for k in range(steps):
            total = base[k]
            for lag in range(k + 1):
                total = total + lags[lag] * signal[k - lag]
            results.append(total)
        return jnp.stack(results).reshape(rows, chan)

    def gate(a, conv):
        base_in, lags_in, base_out, lags_out = conv
        z = convolve(a.astype(bf16), base_in, lags_in).astype(bf16)
        return (z.astype(f32) * convolve(z, base_out, lags_out)).astype(bf16)

    def first_layer(chunk, mine, filters, history):
        blocks, mine_now, filters, history = lax.optimization_barrier(
            (copies(chunk), mine, filters, history)
        )
        gathered = exchange(blocks)
        conv = setup(filters, history)
        other = swap_cores(mine_now)
        weight_in = fetch(core, [mine_now], [other])
        weight_out = fetch(1 - core, [mine_now], [other])
        full = gathered.astype(f32)
        mean_square = jnp.sum(full * full, axis=(0, 2), keepdims=True) / width
        normed = (full * lax.rsqrt(mean_square + 1e-06) * gain_in_all).astype(bf16)
        a = jnp.einsum("trk,tkc->rc", normed, weight_in, preferred_element_type=f32)
        g = gate(a, conv)
        partial = jnp.einsum("rc,tkc->trk", g, weight_out, preferred_element_type=f32)
        summed = jnp.sum(exchange(partial.astype(bf16)).astype(f32), axis=0)
        chunk = (chunk.astype(f32) + gain_out * summed).astype(bf16)
        half = mine[:, : part // 2]
        return chunk, conv, [unset(half)] * 2, [unset(half)] * 2

    def prepare(chunk, mine, filters, history):
        cut = [exchange(mine[:, : part // 2]), exchange(mine[:, part // 2 :])]
        other = [swap_cores(piece) for piece in cut]
        return chunk, setup(filters, history), cut, other

    def later_layer(chunk, conv, cut_in, cut_out):
        values = chunk.astype(f32)
        squares = jnp.sum(values * values, axis=1, keepdims=True)
        scaled = (values * gain_in).astype(bf16)
        partial = jnp.einsum("rk,tkc->trc", scaled, cut_in, preferred_element_type=f32)
        packed = jnp.concatenate([partial.astype(bf16), copies(as_row_pair(squares, chan))], 1)
        totals = jnp.sum(exchange(packed).astype(f32), axis=0)
        square = (totals[rows] + totals[rows + 1])[:rows, None]
        g = gate(totals[:rows] * lax.rsqrt(square / width + 1e-06), conv)
        whole = exchange(copies(g))
        summed = jnp.einsum("trc,tkc->rk", whole, cut_out, preferred_element_type=f32)
        return (values + gain_out * summed).astype(bf16)

    chunk, conv, cut, other = lax.cond(
        plane == 0, first_layer, prepare, chunk, mine, conv_filters[0], conv_caches[0]
    )
    cut_in = fetch(core, cut, other)
    cut_out = fetch(1 - core, cut, other)
    head = pair(lax.dynamic_slice_in_dim(unembed, group * part, part, 0))
    head = jnp.concatenate(head, 1)
    head_gain = lax.dynamic_slice_in_dim(final_gain, group * part, part, 0)
    for layer in range(1, planes):
        chunk = to_plane(chunk, layer - 1, layer)
        chunk = later_layer(chunk, conv, cut_in, cut_out)

    last = planes - 1
    shared = jnp.where(plane == last, chunk, jnp.zeros_like(chunk))
    for target in range(last):
        shared = shared + to_plane(chunk, last, target)
    shared = shared.astype(f32)
    squares = jnp.sum(shared * shared, axis=1, keepdims=True)
    scores = jnp.dot((shared * head_gain).astype(bf16), head, preferred_element_type=f32)
    packed = jnp.concatenate([scores.astype(bf16), as_row_pair(squares, CORES * cols)], 0)
    totals = jnp.sum(exchange(copies(packed)).astype(f32), axis=0)
    square = (totals[rows] + totals[rows + 1])[:rows, None]
    logits = totals[:rows] * lax.rsqrt(square / width + 1e-06)
    kept = jnp.where(core == 0, logits[:, :cols], logits[:, cols:])
    other = swap_cores(jnp.where(core == 0, logits[:, cols:], logits[:, :cols]))
    both = jnp.where(core == 0, jnp.stack([kept, other]), jnp.stack([other, kept]))
    return both.reshape(CORES, steps, own, cols).transpose(1, 0, 2, 3).reshape(steps, requests, cols)


def solution(mesh):
    placed = (
        P(),
        P("section"),
        P("section", None),
        P("section", None, "tensor"),
        P("section", None),
        P("section", None, "tensor"),
        P("section", None, None, "tensor"),
        P(),
        P(None, "section"),
    )
    return jax.shard_map(
        on_device, mesh=mesh, in_specs=placed, out_specs=P(None, None, "section"), check_vma=False
    )
```

```python
import jax
import jax.numpy as jnp
from jax import lax
from jax.experimental import pallas as pl
from jax.experimental.pallas import tpu as pltpu
from jax.sharding import PartitionSpec as P

SHORT = 7
CORES = 2
RECUT = 2
LEAD = 8
EXTRA = 8


def swap_cores(block):
    devices = range(lax.axis_size("section"))
    return lax.ppermute(block, "section", [(i, i ^ 1) for i in devices])


def to_plane(block, source, target):
    route = [(CORES * source + core, CORES * target + core) for core in range(CORES)]
    return lax.ppermute(block, "section", route)


def exchange(blocks):
    return lax.all_to_all(blocks, "tensor", 0, 0)


def copies(block):
    return jnp.broadcast_to(block, (lax.axis_size("tensor"),) + block.shape)


def unset(like):
    return pl.pallas_call(
        lambda out: None,
        out_shape=jax.ShapeDtypeStruct(like.shape, like.dtype),
        out_specs=pl.BlockSpec(memory_space=pl.ANY),
    )()


def terms_kernel(filt_ref, history_ref, out_ref):
    steps = out_ref.shape[0]
    length, requests, chan = history_ref.shape

    def one_position(r, totals):
        row = history_ref[r].astype(jnp.float32)
        return tuple(
            total + filt_ref[pl.ds(LEAD + r - k, 1), :] * row for k, total in enumerate(totals)
        )

    zeros = (jnp.zeros((requests, chan), jnp.float32),) * steps
    totals = lax.fori_loop(0, length, one_position, zeros)
    for k in range(steps):
        out_ref[k] = totals[k]


def cache_terms(filt, history, steps):
    length, requests, chan = history.shape
    padded = jnp.pad(filt[::-1].astype(jnp.float32), ((LEAD, 0), (0, 0)))
    return pl.pallas_call(
        terms_kernel,
        out_shape=jax.ShapeDtypeStruct((steps, requests, chan), jnp.float32),
        in_specs=[pl.BlockSpec(memory_space=pltpu.VMEM)] * 2,
        out_specs=pl.BlockSpec(memory_space=pltpu.VMEM),
        compiler_params=pltpu.CompilerParams(vmem_limit_bytes=8 << 20),
        cost_estimate=pl.CostEstimate(
            flops=2 * steps * requests * length * chan,
            bytes_accessed=2 * requests * length * chan,
            transcendentals=0,
        ),
    )(padded, history)


def stage_kernel(source_ref, out_ref, sem):
    move = pltpu.make_async_copy(source_ref, out_ref, sem)
    move.start()
    move.wait()


def stage(array):
    return pl.pallas_call(
        stage_kernel,
        out_shape=jax.ShapeDtypeStruct(array.shape, array.dtype),
        in_specs=[pl.BlockSpec(memory_space=pl.ANY)],
        out_specs=pl.BlockSpec(memory_space=pltpu.VMEM),
        scratch_shapes=[pltpu.SemaphoreType.DMA],
        compiler_params=pltpu.CompilerParams(vmem_limit_bytes=8 << 20),
    )(array)


def pick(core, arrays, plans, like):
    def kernel(core_ref, *refs):
        sources, out_ref, sems = refs[:-2], refs[-2], refs[-1]
        for c in range(CORES):

            @pl.when(core_ref[0] == c)
            def _():
                moves = [
                    pltpu.make_async_copy(
                        sources[which].at[:, pl.ds(start, size)],
                        out_ref.at[:, pl.ds(place, size)],
                        sems.at[n],
                    )
                    for n, (which, start, place, size) in enumerate(plans[c])
                ]
                for move in moves:
                    move.start()
                for move in moves:
                    move.wait()

    return pl.pallas_call(
        kernel,
        out_shape=jax.ShapeDtypeStruct(like.shape, like.dtype),
        in_specs=[pl.BlockSpec(memory_space=pltpu.SMEM)]
        + [pl.BlockSpec(memory_space=pl.ANY)] * len(arrays),
        out_specs=pl.BlockSpec(memory_space=pltpu.VMEM),
        scratch_shapes=[pltpu.SemaphoreType.DMA((max(map(len, plans)),))],
        compiler_params=pltpu.CompilerParams(vmem_limit_bytes=8 << 20),
    )(core.reshape(1), *arrays)


def even_of(core, mine, other):
    size = mine.shape[1]
    return pick(core, [mine, other], [[(0, 0, 0, size)], [(1, 0, 0, size)]], mine)


def odd_of(core, mine, other):
    return even_of(1 - core, mine, other)


def as_row_pair(column, width):
    row = jnp.pad(column.reshape(1, -1), ((0, 0), (0, width - column.shape[0])))
    high = row.astype(jnp.bfloat16)
    low = (row - high.astype(jnp.float32)).astype(jnp.bfloat16)
    return jnp.pad(jnp.concatenate([high, low], 0), ((0, EXTRA - 2), (0, 0)))


def on_device(
    token_ids,
    block_types,
    embed_table,
    proj_weights,
    norm_gains,
    conv_filters,
    conv_caches,
    final_gain,
    unembed,
):
    f32, bf16 = jnp.float32, jnp.bfloat16
    planes = lax.axis_size("section") // CORES
    section = lax.axis_index("section")
    plane, core = section // CORES, section % CORES
    groups = lax.axis_size("tensor")
    group = lax.axis_index("tensor")
    steps, requests = token_ids.shape
    own = requests // CORES
    rows = steps * own
    vocab_local, width = embed_table.shape
    part = width // groups
    chan = proj_weights.shape[2]
    taps = conv_filters.shape[1]
    cols = unembed.shape[1]

    vocab_ids = section * vocab_local + jnp.arange(vocab_local, dtype=jnp.int32)
    table_part = lax.dynamic_slice_in_dim(embed_table, group * part, part, 1)

    def find(half):
        ids = lax.dynamic_slice_in_dim(token_ids, half * own, own, 1)
        one_hot = (ids[:, :, None] == vocab_ids).astype(bf16).reshape(rows, vocab_local)
        return jnp.dot(one_hot, table_part, preferred_element_type=f32).astype(bf16)

    on_chip = find(core) + swap_cores(find(1 - core))
    on_chip, mine, small = lax.optimization_barrier(
        (
            on_chip,
            proj_weights[0].reshape(groups, part, chan),
            (norm_gains[0], unembed, conv_filters[0], conv_caches[0].transpose(1, 0, 2)),
        )
    )
    my_gain, unembed, filters, history = small

    def pair(mine):
        other = swap_cores(mine)
        even = jnp.where(core == 0, mine, other)
        odd = jnp.where(core == 0, other, mine)
        return even, odd

    chunk = on_chip
    for source in range(1, planes):
        chunk = chunk + to_plane(on_chip, source, 0)
    gain_in, gain_out = pair(my_gain)
    gain_in_all = gain_in.reshape(groups, 1, part)
    gain_in = lax.dynamic_slice_in_dim(gain_in, group * part, part, 0)
    gain_out = lax.dynamic_slice_in_dim(gain_out, group * part, part, 0)

    mask = jnp.where(block_types[0] == 1, 1.0, (jnp.arange(taps) < SHORT).astype(f32))
    filt = filters.astype(f32) * mask[:, None]
    terms = cache_terms(filt, history, steps).reshape(steps, CORES, own, chan)
    terms_kept = lax.dynamic_index_in_dim(terms, core, 1, keepdims=False)
    terms_given = lax.dynamic_index_in_dim(terms, 1 - core, 1, keepdims=False)
    terms_other = swap_cores(terms_given)
    base_in = jnp.where(core == 0, terms_kept, terms_other)
    base_out = jnp.where(core == 0, terms_other, terms_kept)
    lags_in, lags_out = pair(filt[:steps])
    theirs = swap_cores(mine)

    def convolve(signal, base, lags):
        signal = signal.astype(f32).reshape(steps, own, chan)
        results = []
        for k in range(steps):
            total = base[k]
            for lag in range(k + 1):
                total = total + lags[lag] * signal[k - lag]
            results.append(total)
        return jnp.stack(results).reshape(rows, chan)

    def gate(a):
        z = convolve(a.astype(bf16), base_in, lags_in).astype(bf16)
        return (z.astype(f32) * convolve(z, base_out, lags_out)).astype(bf16)

    def first_plane(chunk, mine, theirs):
        weight_in, weight_out = even_of(core, mine, theirs), odd_of(core, mine, theirs)
        return native_layer(chunk, weight_in, weight_out), unset(mine), unset(mine)

    def second_plane(chunk, mine, theirs):
        half = part // 2
        plans = [[(0, 0, 0, half)], [(1, half, 0, half)]]
        piece = exchange(pick(core, [mine, theirs], plans, mine[:, :half]))
        plans = [[(0, 0, 0, half), (1, 0, half, half)], [(1, 0, 0, half), (0, 0, half, half)]]
        cut_in = pick(core, [piece, swap_cores(piece)], plans, mine)
        return chunk, cut_in, odd_of(core, mine, theirs)

    def last_planes(chunk, mine, theirs):
        cut = exchange(stage(mine))
        other = swap_cores(cut)
        return chunk, even_of(core, cut, other), odd_of(core, cut, other)

    def project_in(chunk, cut_in):
        values = chunk.astype(f32)
        squares = jnp.sum(values * values, axis=1, keepdims=True)
        scaled = (values * gain_in).astype(bf16)
        partial = jnp.einsum("rk,tkc->trc", scaled, cut_in, preferred_element_type=f32)
        packed = jnp.concatenate([partial.astype(bf16), copies(as_row_pair(squares, chan))], 1)
        totals = jnp.sum(exchange(packed).astype(f32), axis=0)
        square = (totals[rows] + totals[rows + 1])[:rows, None]
        return gate(totals[:rows] * lax.rsqrt(square / width + 1e-06))

    def project_out(chunk, g, weight_out):
        partial = jnp.einsum("rc,tkc->trk", g, weight_out, preferred_element_type=f32)
        summed = jnp.sum(exchange(partial.astype(bf16)).astype(f32), axis=0)
        return (chunk.astype(f32) + gain_out * summed).astype(bf16)

    def native_layer(chunk, weight_in, weight_out):
        full = exchange(copies(chunk)).astype(f32)
        mean_square = jnp.sum(full * full, axis=(0, 2), keepdims=True) / width
        normed = (full * lax.rsqrt(mean_square + 1e-06) * gain_in_all).astype(bf16)
        g = gate(jnp.einsum("trk,tkc->rc", normed, weight_in, preferred_element_type=f32))
        return project_out(chunk, g, weight_out)

    def half_cut_layer(chunk, cut_in, weight_out):
        return project_out(chunk, project_in(chunk, cut_in), weight_out)

    def cut_layer(chunk, cut_in, cut_out):
        whole = exchange(copies(project_in(chunk, cut_in)))
        summed = jnp.einsum("trc,tkc->rk", whole, cut_out, preferred_element_type=f32)
        return (chunk.astype(f32) + gain_out * summed).astype(bf16)

    chunk, weight_in, weight_out = lax.switch(
        jnp.minimum(plane, RECUT), [first_plane, second_plane, last_planes], chunk, mine, theirs
    )
    chunk = to_plane(chunk, 0, 1)
    chunk, weight_in, weight_out, unembed = lax.optimization_barrier(
        (chunk, weight_in, weight_out, unembed)
    )
    chunk = lax.cond(plane == 1, half_cut_layer, lambda c, a, b: c, chunk, weight_in, weight_out)
    for layer in range(RECUT, planes):
        chunk = to_plane(chunk, layer - 1, layer)
        chunk = cut_layer(chunk, weight_in, weight_out)
    head = pair(lax.dynamic_slice_in_dim(unembed, group * part, part, 0))
    head = jnp.concatenate(head, 1)
    head_gain = lax.dynamic_slice_in_dim(final_gain, group * part, part, 0)

    last = planes - 1
    shared = jnp.where(plane == last, chunk, jnp.zeros_like(chunk))
    for target in range(last):
        shared = shared + to_plane(chunk, last, target)
    shared = shared.astype(f32)
    squares = jnp.sum(shared * shared, axis=1, keepdims=True)
    scores = jnp.dot((shared * head_gain).astype(bf16), head, preferred_element_type=f32)
    packed = jnp.concatenate([scores.astype(bf16), as_row_pair(squares, CORES * cols)], 0)
    totals = jnp.sum(exchange(copies(packed)).astype(f32), axis=0)
    square = (totals[rows] + totals[rows + 1])[:rows, None]
    logits = totals[:rows] * lax.rsqrt(square / width + 1e-06)
    kept = jnp.where(core == 0, logits[:, :cols], logits[:, cols:])
    other = swap_cores(jnp.where(core == 0, logits[:, cols:], logits[:, :cols]))
    both = jnp.where(core == 0, jnp.stack([kept, other]), jnp.stack([other, kept]))
    return both.reshape(CORES, steps, own, cols).transpose(1, 0, 2, 3).reshape(steps, requests, cols)


def solution(mesh):
    placed = (
        P(),
        P("section"),
        P("section", None),
        P("section", None, "tensor"),
        P("section", None),
        P("section", None, "tensor"),
        P("section", None, None, "tensor"),
        P(),
        P(None, "section"),
    )
    return jax.shard_map(
        on_device, mesh=mesh, in_specs=placed, out_specs=P(None, None, "section"), check_vma=False
    )
```

```python
import functools

import jax
import jax.numpy as jnp
from jax import lax
from jax.experimental import pallas as pl
from jax.experimental.pallas import tpu as pltpu
from jax.sharding import PartitionSpec as P

SHORT = 7
CORES = 2
RECUT = 2
PARTS = 4
PIECES = 4
CORE, GROUP, KIND = range(3)
EXTRA = 16


def swap_cores(block):
    devices = range(lax.axis_size("section"))
    return lax.ppermute(block, "section", [(i, i ^ 1) for i in devices])


def to_plane(block, source, target):
    route = [(CORES * source + core, CORES * target + core) for core in range(CORES)]
    return lax.ppermute(block, "section", route)


def from_plane_behind(block, distance):
    devices = lax.axis_size("section")
    route = [(i, (i + CORES * distance) % devices) for i in range(devices)]
    return lax.ppermute(block, "section", route)


def exchange(blocks):
    return lax.all_to_all(blocks, "tensor", 0, 0)


def copies(block):
    return jnp.broadcast_to(block, (lax.axis_size("tensor"),) + block.shape)


def unset(like):
    return pl.pallas_call(
        lambda out: None,
        out_shape=jax.ShapeDtypeStruct(like.shape, like.dtype),
        out_specs=pl.BlockSpec(memory_space=pl.ANY),
    )()


def on_vmem(kernel, shapes, scratch=(), cost=0):
    def call(flags, *arrays):
        return pl.pallas_call(
            kernel,
            out_shape=shapes,
            in_specs=[pl.BlockSpec(memory_space=pltpu.SMEM)]
            + [pl.BlockSpec(memory_space=pltpu.VMEM)] * len(arrays),
            out_specs=jax.tree.map(lambda _: pl.BlockSpec(memory_space=pltpu.VMEM), shapes),
            scratch_shapes=list(scratch),
            compiler_params=pltpu.CompilerParams(vmem_limit_bytes=24 << 20),
            cost_estimate=pl.CostEstimate(
                flops=cost,
                bytes_accessed=sum(a.size * a.dtype.itemsize for a in arrays),
                transcendentals=0,
            ),
        )(flags, *arrays)

    return call


def shape(dims, dtype=jnp.bfloat16):
    return jax.ShapeDtypeStruct(dims, dtype)


def terms_kernel(flags_ref, filt_ref, history_ref, kept_ref, given_ref, taps_ref):
    steps = kept_ref.shape[0]
    own = kept_ref.shape[1] - EXTRA
    taps, chan = filt_ref.shape
    length, requests, _ = history_ref.shape
    place = lax.broadcasted_iota(jnp.int32, (taps, chan), 0)
    used = (place < SHORT) | (flags_ref[KIND] == 1)
    taps_ref[0:taps] = jnp.where(used, filt_ref[...].astype(jnp.float32), 0.0)
    taps_ref[taps:] = jnp.zeros((EXTRA, chan), jnp.float32)

    def one_position(r, totals):
        row = history_ref[r].astype(jnp.float32)
        return tuple(
            total + taps_ref[pl.ds(taps - 1 + k - r, 1), :] * row for k, total in enumerate(totals)
        )

    zeros = (jnp.zeros((requests, chan), jnp.float32),) * steps
    totals = lax.fori_loop(0, length, one_position, zeros)
    first = flags_ref[CORE] == 0
    for k in range(steps):
        low, high = totals[k][:own], totals[k][own:]
        kept_ref[k, 0:own] = jnp.where(first, low, high)
        given_ref[k, 0:own] = jnp.where(first, high, low)
        lag = jnp.broadcast_to(taps_ref[k : k + 1, :], (EXTRA, chan))
        kept_ref[k, own:] = lag
        given_ref[k, own:] = lag


def cache_terms(flags, filters, history, steps):
    taps, chan = filters.shape
    length, requests, _ = history.shape
    out = shape((steps, requests // CORES + EXTRA, chan), jnp.float32)
    scratch = [pltpu.VMEM((taps + EXTRA, chan), jnp.float32)]
    cost = 2 * steps * requests * length * chan
    return on_vmem(terms_kernel, [out, out], scratch, cost)(flags, filters, history)


def gate(flags_ref, kept_ref, received_ref, a):
    steps = kept_ref.shape[0]
    own = kept_ref.shape[1] - EXTRA
    first = flags_ref[CORE] == 0

    def convolve(even, signal):
        results = []
        for k in range(steps):
            total = None
            for lag in range(k, -1, -1):
                mine, other = kept_ref[lag], received_ref[lag]
                terms = jnp.where(first, mine, other) if even else jnp.where(first, other, mine)
                if lag == k:
                    mine, other = kept_ref[k], received_ref[k]
                    base = jnp.where(first, mine, other) if even else jnp.where(first, other, mine)
                    total = base[:own]
                total = total + terms[own : own + 1] * signal[k - lag]
            results.append(total)
        return results

    a = a.astype(jnp.bfloat16).astype(jnp.float32)
    z = convolve(True, [a[k * own : (k + 1) * own] for k in range(steps)])
    z = [part.astype(jnp.bfloat16).astype(jnp.float32) for part in z]
    mixed = convolve(False, z)
    return jnp.concatenate([x * y for x, y in zip(z, mixed)], 0).astype(jnp.bfloat16)


def dot(x, y):
    return jnp.dot(x, y, preferred_element_type=jnp.float32)


def dot_turned(x, y):
    return lax.dot_general(x, y, (((1,), (1,)), ((), ())), preferred_element_type=jnp.float32)


def gain_part(flags_ref, mine_ref, other_ref, even, start, size):
    mine, other = mine_ref[:, pl.ds(start, size)], other_ref[:, pl.ds(start, size)]
    first = flags_ref[CORE] == 0
    return jnp.where(first, mine, other) if even else jnp.where(first, other, mine)


def spread_kernel(flags_ref, *refs):
    parts, (sum_ref, out_ref) = refs[:PARTS], refs[-2:]
    total = parts[0][...].astype(jnp.float32)
    for part_ref in parts[1:]:
        total = total + part_ref[...].astype(jnp.float32)
    total = total.astype(jnp.bfloat16)
    sum_ref[...] = total
    for t in range(out_ref.shape[0]):
        out_ref[t] = total


def native_kernel(
    flags_ref,
    full_ref,
    gain_ref,
    gain2_ref,
    kept_ref,
    received_ref,
    mine_ref,
    other_ref,
    out_ref,
    in_buffer,
    back_buffer,
    sems,
):
    groups, rows, part = full_ref.shape
    chan = mine_ref.shape[2]

    def moves(source_ref, buffer_ref, first):
        size = groups // PIECES
        return [
            pltpu.make_async_copy(
                source_ref.at[pl.ds(n * size, size)],
                buffer_ref.at[pl.ds(n * size, size)],
                sems.at[first + n],
            )
            for n in range(PIECES)
        ]

    for core in range(CORES):
        in_ref, back_ref = (mine_ref, other_ref) if core == 0 else (other_ref, mine_ref)

        @pl.when(flags_ref[CORE] == core)
        def _():
            ahead = moves(in_ref, in_buffer, 0)
            after = moves(back_ref, back_buffer, PIECES)
            for move in ahead:
                move.start()
            squares = jnp.zeros((rows, 1), jnp.float32)
            for t in range(groups):
                values = full_ref[t].astype(jnp.float32)
                squares = squares + jnp.sum(values * values, axis=1, keepdims=True)
            scale = lax.rsqrt(squares / (groups * part) + 1e-06)
            a = jnp.zeros((rows, chan), jnp.float32)
            for t in range(groups):
                gain = gain_part(flags_ref, gain_ref, gain2_ref, True, t * part, part)
                normed = full_ref[t].astype(jnp.float32) * scale * gain
                if t % (groups // PIECES) == 0:
                    ahead[t // (groups // PIECES)].wait()
                if t == 0:
                    for move in after:
                        move.start()
                a = a + dot(normed.astype(jnp.bfloat16), in_buffer[t])
            g = gate(flags_ref, kept_ref, received_ref, a)
            for t in range(groups):
                if t % (groups // PIECES) == 0:
                    after[t // (groups // PIECES)].wait()
                out_ref[t] = dot_turned(g, back_buffer[t]).astype(jnp.bfloat16)


def residual_kernel(flags_ref, arrived_ref, chunk_ref, gain_ref, gain2_ref, out_ref):
    groups, rows, part = arrived_ref.shape
    start = pl.multiple_of(flags_ref[GROUP] * part, part)
    gain = gain_part(flags_ref, gain_ref, gain2_ref, False, start, part)
    summed = arrived_ref[0].astype(jnp.float32)
    for t in range(1, groups):
        summed = summed + arrived_ref[t].astype(jnp.float32)
    out_ref[...] = (chunk_ref[...].astype(jnp.float32) + gain * summed).astype(jnp.bfloat16)


def in_kernel(flags_ref, chunk_ref, gain_ref, gain2_ref, cut_ref, out_ref):
    groups, part, chan = cut_ref.shape
    rows = chunk_ref.shape[0]
    start = pl.multiple_of(flags_ref[GROUP] * part, part)
    gain = gain_part(flags_ref, gain_ref, gain2_ref, True, start, part)
    values = chunk_ref[...].astype(jnp.float32)
    scaled = (values * gain).astype(jnp.bfloat16)
    column = jnp.sum(values * values, axis=1, keepdims=True)
    diagonal = lax.broadcasted_iota(jnp.int32, (rows, chan), 0) == lax.broadcasted_iota(
        jnp.int32, (rows, chan), 1
    )
    row = jnp.sum(jnp.where(diagonal, column, 0.0), axis=0, keepdims=True)
    high = row.astype(jnp.bfloat16).astype(jnp.float32)
    below = lax.broadcasted_iota(jnp.int32, (EXTRA, chan), 0)
    pair = jnp.where(below == 0, high, jnp.where(below == 1, row - high, 0.0))
    pair = pair.astype(jnp.bfloat16)
    for t in range(groups):
        out_ref[t, 0:rows] = dot(scaled, cut_ref[t]).astype(jnp.bfloat16)
        out_ref[t, rows:] = pair


def gated(flags_ref, arrived_ref, kept_ref, received_ref, width):
    groups, rows, chan = arrived_ref.shape
    rows = rows - EXTRA
    totals = arrived_ref[0].astype(jnp.float32)
    for t in range(1, groups):
        totals = totals + arrived_ref[t].astype(jnp.float32)
    row = totals[rows : rows + 1] + totals[rows + 1 : rows + 2]
    diagonal = lax.broadcasted_iota(jnp.int32, (rows, chan), 0) == lax.broadcasted_iota(
        jnp.int32, (rows, chan), 1
    )
    squares = jnp.sum(jnp.where(diagonal, row, 0.0), axis=1, keepdims=True)
    return gate(
        flags_ref, kept_ref, received_ref, totals[:rows] * lax.rsqrt(squares / width + 1e-06)
    )


def gate_kernel(flags_ref, arrived_ref, kept_ref, received_ref, out_ref, *, width):
    g = gated(flags_ref, arrived_ref, kept_ref, received_ref, width)
    for t in range(out_ref.shape[0]):
        out_ref[t] = g


def gate_out_kernel(flags_ref, arrived_ref, kept_ref, received_ref, back_ref, out_ref, *, width):
    g = gated(flags_ref, arrived_ref, kept_ref, received_ref, width)
    for t in range(out_ref.shape[0]):
        out_ref[t] = dot_turned(g, back_ref[t]).astype(jnp.bfloat16)


def out_kernel(flags_ref, whole_ref, chunk_ref, gain_ref, gain2_ref, cut_ref, out_ref):
    groups, part, chan = cut_ref.shape
    start = pl.multiple_of(flags_ref[GROUP] * part, part)
    gain = gain_part(flags_ref, gain_ref, gain2_ref, False, start, part)
    summed = dot_turned(whole_ref[0], cut_ref[0])
    for t in range(1, groups):
        summed = summed + dot_turned(whole_ref[t], cut_ref[t])
    out_ref[...] = (chunk_ref[...].astype(jnp.float32) + gain * summed).astype(jnp.bfloat16)


def stage_kernel(source_ref, out_ref, sem):
    move = pltpu.make_async_copy(source_ref, out_ref, sem)
    move.start()
    move.wait()


def stage(array):
    return pl.pallas_call(
        stage_kernel,
        out_shape=jax.ShapeDtypeStruct(array.shape, array.dtype),
        in_specs=[pl.BlockSpec(memory_space=pl.ANY)],
        out_specs=pl.BlockSpec(memory_space=pltpu.VMEM),
        scratch_shapes=[pltpu.SemaphoreType.DMA],
        compiler_params=pltpu.CompilerParams(vmem_limit_bytes=8 << 20),
    )(array)


def pick(core, arrays, plans, like):
    def kernel(core_ref, *refs):
        sources, out_ref, sems = refs[:-2], refs[-2], refs[-1]
        for c in range(CORES):

            @pl.when(core_ref[0] == c)
            def _():
                moves = [
                    pltpu.make_async_copy(
                        sources[which].at[:, pl.ds(start, size)],
                        out_ref.at[:, pl.ds(place, size)],
                        sems.at[n],
                    )
                    for n, (which, start, place, size) in enumerate(plans[c])
                ]
                for move in moves:
                    move.start()
                for move in moves:
                    move.wait()

    return pl.pallas_call(
        kernel,
        out_shape=jax.ShapeDtypeStruct(like.shape, like.dtype),
        in_specs=[pl.BlockSpec(memory_space=pltpu.SMEM)]
        + [pl.BlockSpec(memory_space=pl.ANY)] * len(arrays),
        out_specs=pl.BlockSpec(memory_space=pltpu.VMEM),
        scratch_shapes=[pltpu.SemaphoreType.DMA((max(map(len, plans)),))],
        compiler_params=pltpu.CompilerParams(vmem_limit_bytes=8 << 20),
    )(core.reshape(1), *arrays)


def even_of(core, mine, other):
    size = mine.shape[1]
    return pick(core, [mine, other], [[(0, 0, 0, size)], [(1, 0, 0, size)]], mine)


def odd_of(core, mine, other):
    return even_of(1 - core, mine, other)


def as_row_pair(column, width):
    row = jnp.pad(column.reshape(1, -1), ((0, 0), (0, width - column.shape[0])))
    high = row.astype(jnp.bfloat16)
    low = (row - high.astype(jnp.float32)).astype(jnp.bfloat16)
    return jnp.pad(jnp.concatenate([high, low], 0), ((0, EXTRA - 2), (0, 0)))


def on_device(
    token_ids,
    block_types,
    embed_table,
    proj_weights,
    norm_gains,
    conv_filters,
    conv_caches,
    final_gain,
    unembed,
):
    f32, bf16 = jnp.float32, jnp.bfloat16
    planes = lax.axis_size("section") // CORES
    section = lax.axis_index("section")
    plane, core = section // CORES, section % CORES
    groups = lax.axis_size("tensor")
    group = lax.axis_index("tensor")
    steps, requests = token_ids.shape
    own = requests // CORES
    rows = steps * own
    vocab_local, width = embed_table.shape
    part = width // groups
    chan = proj_weights.shape[2]
    cols = unembed.shape[1]

    vocab_ids = section * vocab_local + jnp.arange(vocab_local, dtype=jnp.int32)
    table_part = lax.dynamic_slice_in_dim(embed_table, group * part, part, 1)

    def find(half):
        ids = lax.dynamic_slice_in_dim(token_ids, half * own, own, 1)
        one_hot = (ids[:, :, None] == vocab_ids).astype(bf16).reshape(rows, vocab_local)
        return jnp.dot(one_hot, table_part, preferred_element_type=f32).astype(bf16)

    on_chip = find(core) + swap_cores(find(1 - core))
    flags = jnp.stack([core, group, block_types[0]]).astype(jnp.int32)
    on_chip, flags, mine, gains, filters, history, unembed = lax.optimization_barrier(
        (
            on_chip,
            flags,
            proj_weights[0].reshape(groups, part, chan),
            norm_gains,
            conv_filters[0],
            conv_caches[0].transpose(1, 0, 2),
            unembed,
        )
    )
    theirs, gains2 = swap_cores(mine), swap_cores(gains)

    arriving = [from_plane_behind(on_chip, distance) for distance in range(1, planes)]

    work = 2 * rows * width * chan
    wide = shape((groups, rows, part))
    packed_shape = shape((groups, rows + EXTRA, chan))

    def prepare_terms(filters, history):
        kept, given = cache_terms(flags, filters, history, steps)
        return kept, swap_cores(given)

    def add_exchanged(chunk, blocks):
        return on_vmem(residual_kernel, shape((rows, part)))(
            flags, exchange(blocks), chunk, gains, gains2
        )

    def project_in(chunk, cut_in):
        kernel = on_vmem(in_kernel, packed_shape, cost=work)
        return exchange(kernel(flags, chunk, gains, gains2, cut_in))

    def first_plane(on_chip, arriving, mine, theirs, filters, history):
        chunk, blocks = on_vmem(spread_kernel, [shape((rows, part)), wide])(
            flags, on_chip, *arriving
        )
        blocks, filters, history, mine, theirs = lax.optimization_barrier(
            (blocks, filters, history, mine, theirs)
        )
        full = exchange(blocks)
        kept, received = prepare_terms(filters, history)
        blocks = pl.pallas_call(
            native_kernel,
            out_shape=wide,
            in_specs=[pl.BlockSpec(memory_space=pltpu.SMEM)]
            + [pl.BlockSpec(memory_space=pltpu.VMEM)] * 5
            + [pl.BlockSpec(memory_space=pl.ANY)] * 2,
            out_specs=pl.BlockSpec(memory_space=pltpu.VMEM),
            scratch_shapes=[pltpu.VMEM(mine.shape, bf16)] * 2
            + [pltpu.SemaphoreType.DMA((2 * PIECES,))],
            compiler_params=pltpu.CompilerParams(vmem_limit_bytes=24 << 20),
        )(flags, full, gains, gains2, kept, received, mine, theirs)
        return add_exchanged(chunk, blocks), unset(mine), unset(mine), unset(kept), unset(kept)

    def second_plane(chunk, arriving, mine, theirs, filters, history):
        half = part // 2
        plans = [[(0, 0, 0, half)], [(1, half, 0, half)]]
        piece = exchange(pick(core, [mine, theirs], plans, mine[:, :half]))
        plans = [[(0, 0, 0, half), (1, 0, half, half)], [(1, 0, 0, half), (0, 0, half, half)]]
        cut_in = pick(core, [piece, swap_cores(piece)], plans, mine)
        return chunk, cut_in, odd_of(core, mine, theirs), *prepare_terms(filters, history)

    def last_planes(chunk, arriving, mine, theirs, filters, history):
        cut = exchange(stage(mine))
        other = swap_cores(cut)
        weights = even_of(core, cut, other), odd_of(core, cut, other)
        return chunk, *weights, *prepare_terms(filters, history)

    def half_cut_layer(chunk, cut_in, weight_out, kept, received):
        arrived = project_in(chunk, cut_in)
        kernel = functools.partial(gate_out_kernel, width=width)
        kernel = on_vmem(kernel, wide, cost=work)
        return add_exchanged(chunk, kernel(flags, arrived, kept, received, weight_out))

    def cut_layer(chunk, cut_in, cut_out, kept, received):
        arrived = project_in(chunk, cut_in)
        kernel = on_vmem(functools.partial(gate_kernel, width=width), shape((groups, rows, chan)))
        whole = exchange(kernel(flags, arrived, kept, received))
        return on_vmem(out_kernel, shape((rows, part)), cost=work)(
            flags, whole, chunk, gains, gains2, cut_out
        )

    chunk, *held = lax.switch(
        jnp.minimum(plane, RECUT),
        [first_plane, second_plane, last_planes],
        on_chip,
        arriving,
        mine,
        theirs,
        filters,
        history,
    )
    chunk, unembed, final_gain = lax.optimization_barrier((chunk, unembed, final_gain))
    other_head = swap_cores(lax.dynamic_slice_in_dim(unembed, group * part, part, 0))
    my_head = lax.dynamic_slice_in_dim(unembed, group * part, part, 0)
    head = jnp.where(
        core == 0,
        jnp.concatenate([my_head, other_head], 1),
        jnp.concatenate([other_head, my_head], 1),
    )
    head_gain = lax.dynamic_slice_in_dim(final_gain, group * part, part, 0)
    chunk = to_plane(chunk, 0, 1)
    chunk, held, head, head_gain = lax.optimization_barrier((chunk, held, head, head_gain))
    chunk = lax.cond(plane == 1, half_cut_layer, lambda c, *held: c, chunk, *held)
    staged = stage(lax.optimization_barrier((chunk, held[0]))[1])
    for layer in range(RECUT, planes):
        chunk = to_plane(chunk, layer - 1, layer)
        if layer == RECUT:
            chunk, staged = lax.optimization_barrier((chunk, staged))
        first = staged if layer == RECUT else held[0]
        chunk = cut_layer(chunk, first, *held[1:])
    last = planes - 1
    shared = jnp.where(plane == last, chunk, jnp.zeros_like(chunk))
    for target in range(last):
        shared = shared + to_plane(chunk, last, target)
    shared = shared.astype(f32)
    squares = jnp.sum(shared * shared, axis=1, keepdims=True)
    scores = jnp.dot((shared * head_gain).astype(bf16), head, preferred_element_type=f32)
    packed = jnp.concatenate([scores.astype(bf16), as_row_pair(squares, CORES * cols)], 0)
    totals = jnp.sum(exchange(copies(packed)).astype(f32), axis=0)
    square = (totals[rows] + totals[rows + 1])[:rows, None]
    logits = totals[:rows] * lax.rsqrt(square / width + 1e-06)
    kept = jnp.where(core == 0, logits[:, :cols], logits[:, cols:])
    other = swap_cores(jnp.where(core == 0, logits[:, cols:], logits[:, :cols]))
    both = jnp.where(core == 0, jnp.stack([kept, other]), jnp.stack([other, kept]))
    return both.reshape(CORES, steps, own, cols).transpose(1, 0, 2, 3).reshape(steps, requests, cols)


def solution(mesh):
    placed = (
        P(),
        P("section"),
        P("section", None),
        P("section", None, "tensor"),
        P("section", None),
        P("section", None, "tensor"),
        P("section", None, None, "tensor"),
        P(),
        P(None, "section"),
    )
    return jax.shard_map(
        on_device, mesh=mesh, in_specs=placed, out_specs=P(None, None, "section"), check_vma=False
    )
```

```python
import functools

import jax
import jax.numpy as jnp
from jax import lax
from jax.experimental import pallas as pl
from jax.experimental.pallas import tpu as pltpu
from jax.sharding import PartitionSpec as P

SHORT = 7
CORES = 2
RECUT = 2
PARTS = 4
PIECES = 4
CORE, GROUP, KIND = range(3)
EXTRA = 16


def swap_cores(block):
    devices = range(lax.axis_size("section"))
    return lax.ppermute(block, "section", [(i, i ^ 1) for i in devices])


def to_plane(block, source, target):
    route = [(CORES * source + core, CORES * target + core) for core in range(CORES)]
    return lax.ppermute(block, "section", route)


def from_plane_behind(block, distance):
    devices = lax.axis_size("section")
    route = [(i, (i + CORES * distance) % devices) for i in range(devices)]
    return lax.ppermute(block, "section", route)


def exchange(blocks):
    return lax.all_to_all(blocks, "tensor", 0, 0)


def copies(block):
    return jnp.broadcast_to(block, (lax.axis_size("tensor"),) + block.shape)


def unset(like):
    return pl.pallas_call(
        lambda out: None,
        out_shape=jax.ShapeDtypeStruct(like.shape, like.dtype),
        out_specs=pl.BlockSpec(memory_space=pl.ANY),
    )()


def on_vmem(kernel, shapes, scratch=(), cost=0):
    def call(flags, *arrays):
        return pl.pallas_call(
            kernel,
            out_shape=shapes,
            in_specs=[pl.BlockSpec(memory_space=pltpu.SMEM)]
            + [pl.BlockSpec(memory_space=pltpu.VMEM)] * len(arrays),
            out_specs=jax.tree.map(lambda _: pl.BlockSpec(memory_space=pltpu.VMEM), shapes),
            scratch_shapes=list(scratch),
            compiler_params=pltpu.CompilerParams(vmem_limit_bytes=24 << 20),
            cost_estimate=pl.CostEstimate(
                flops=cost,
                bytes_accessed=sum(a.size * a.dtype.itemsize for a in arrays),
                transcendentals=0,
            ),
        )(flags, *arrays)

    return call


def shape(dims, dtype=jnp.bfloat16):
    return jax.ShapeDtypeStruct(dims, dtype)


def terms_kernel(flags_ref, filt_ref, history_ref, kept_ref, given_ref, taps_ref):
    steps = kept_ref.shape[0]
    own = kept_ref.shape[1] - EXTRA
    taps, chan = filt_ref.shape
    length, requests, _ = history_ref.shape
    place = lax.broadcasted_iota(jnp.int32, (taps, chan), 0)
    used = (place < SHORT) | (flags_ref[KIND] == 1)
    taps_ref[0:taps] = jnp.where(used, filt_ref[...].astype(jnp.float32), 0.0)
    taps_ref[taps:] = jnp.zeros((EXTRA, chan), jnp.float32)

    def one_position(r, totals):
        row = history_ref[r].astype(jnp.float32)
        return tuple(
            total + taps_ref[pl.ds(taps - 1 + k - r, 1), :] * row for k, total in enumerate(totals)
        )

    zeros = (jnp.zeros((requests, chan), jnp.float32),) * steps
    totals = lax.fori_loop(0, length, one_position, zeros)
    first = flags_ref[CORE] == 0
    for k in range(steps):
        low, high = totals[k][:own], totals[k][own:]
        kept_ref[k, 0:own] = jnp.where(first, low, high)
        given_ref[k, 0:own] = jnp.where(first, high, low)
        lag = jnp.broadcast_to(taps_ref[k : k + 1, :], (EXTRA, chan))
        kept_ref[k, own:] = lag
        given_ref[k, own:] = lag


def cache_terms(flags, filters, history, steps):
    taps, chan = filters.shape
    length, requests, _ = history.shape
    out = shape((steps, requests // CORES + EXTRA, chan), jnp.float32)
    scratch = [pltpu.VMEM((taps + EXTRA, chan), jnp.float32)]
    cost = 2 * steps * requests * length * chan
    return on_vmem(terms_kernel, [out, out], scratch, cost)(flags, filters, history)


def gate(flags_ref, kept_ref, received_ref, a):
    steps = kept_ref.shape[0]
    own = kept_ref.shape[1] - EXTRA
    first = flags_ref[CORE] == 0

    def convolve(even, signal):
        results = []
        for k in range(steps):
            total = None
            for lag in range(k, -1, -1):
                mine, other = kept_ref[lag], received_ref[lag]
                terms = jnp.where(first, mine, other) if even else jnp.where(first, other, mine)
                if lag == k:
                    mine, other = kept_ref[k], received_ref[k]
                    base = jnp.where(first, mine, other) if even else jnp.where(first, other, mine)
                    total = base[:own]
                total = total + terms[own : own + 1] * signal[k - lag]
            results.append(total)
        return results

    a = a.astype(jnp.bfloat16).astype(jnp.float32)
    z = convolve(True, [a[k * own : (k + 1) * own] for k in range(steps)])
    z = [part.astype(jnp.bfloat16).astype(jnp.float32) for part in z]
    mixed = convolve(False, z)
    return jnp.concatenate([x * y for x, y in zip(z, mixed)], 0).astype(jnp.bfloat16)


def dot(x, y):
    return jnp.dot(x, y, preferred_element_type=jnp.float32)


def dot_turned(x, y):
    return lax.dot_general(x, y, (((1,), (1,)), ((), ())), preferred_element_type=jnp.float32)


def gain_part(flags_ref, mine_ref, other_ref, even, start, size):
    mine, other = mine_ref[:, pl.ds(start, size)], other_ref[:, pl.ds(start, size)]
    first = flags_ref[CORE] == 0
    return jnp.where(first, mine, other) if even else jnp.where(first, other, mine)


def spread_kernel(flags_ref, *refs):
    parts, (sum_ref, out_ref) = refs[:PARTS], refs[-2:]
    total = parts[0][...].astype(jnp.float32)
    for part_ref in parts[1:]:
        total = total + part_ref[...].astype(jnp.float32)
    total = total.astype(jnp.bfloat16)
    sum_ref[...] = total
    for t in range(out_ref.shape[0]):
        out_ref[t] = total


def native_kernel(
    flags_ref,
    full_ref,
    gain_ref,
    gain2_ref,
    kept_ref,
    received_ref,
    mine_ref,
    other_ref,
    out_ref,
    in_buffer,
    back_buffer,
    sems,
):
    groups, rows, part = full_ref.shape
    chan = mine_ref.shape[2]

    def moves(source_ref, buffer_ref, first):
        size = groups // PIECES
        return [
            pltpu.make_async_copy(
                source_ref.at[pl.ds(n * size, size)],
                buffer_ref.at[pl.ds(n * size, size)],
                sems.at[first + n],
            )
            for n in range(PIECES)
        ]

    for core in range(CORES):
        in_ref, back_ref = (mine_ref, other_ref) if core == 0 else (other_ref, mine_ref)

        @pl.when(flags_ref[CORE] == core)
        def _():
            ahead = moves(in_ref, in_buffer, 0)
            after = moves(back_ref, back_buffer, PIECES)
            for move in ahead:
                move.start()
            squares = jnp.zeros((rows, 1), jnp.float32)
            for t in range(groups):
                values = full_ref[t].astype(jnp.float32)
                squares = squares + jnp.sum(values * values, axis=1, keepdims=True)
            scale = lax.rsqrt(squares / (groups * part) + 1e-06)
            a = jnp.zeros((rows, chan), jnp.float32)
            for t in range(groups):
                gain = gain_part(flags_ref, gain_ref, gain2_ref, True, t * part, part)
                normed = full_ref[t].astype(jnp.float32) * scale * gain
                if t % (groups // PIECES) == 0:
                    ahead[t // (groups // PIECES)].wait()
                if t == 0:
                    for move in after:
                        move.start()
                a = a + dot(normed.astype(jnp.bfloat16), in_buffer[t])
            g = gate(flags_ref, kept_ref, received_ref, a)
            for t in range(groups):
                if t % (groups // PIECES) == 0:
                    after[t // (groups // PIECES)].wait()
                out_ref[t] = dot_turned(g, back_buffer[t]).astype(jnp.bfloat16)


def residual_kernel(flags_ref, arrived_ref, chunk_ref, gain_ref, gain2_ref, out_ref):
    groups, rows, part = arrived_ref.shape
    start = pl.multiple_of(flags_ref[GROUP] * part, part)
    gain = gain_part(flags_ref, gain_ref, gain2_ref, False, start, part)
    summed = arrived_ref[0].astype(jnp.float32)
    for t in range(1, groups):
        summed = summed + arrived_ref[t].astype(jnp.float32)
    out_ref[...] = (chunk_ref[...].astype(jnp.float32) + gain * summed).astype(jnp.bfloat16)


def in_kernel(flags_ref, chunk_ref, gain_ref, gain2_ref, cut_ref, out_ref):
    groups, part, chan = cut_ref.shape
    rows = chunk_ref.shape[0]
    start = pl.multiple_of(flags_ref[GROUP] * part, part)
    gain = gain_part(flags_ref, gain_ref, gain2_ref, True, start, part)
    values = chunk_ref[...].astype(jnp.float32)
    scaled = (values * gain).astype(jnp.bfloat16)
    column = jnp.sum(values * values, axis=1, keepdims=True)
    diagonal = lax.broadcasted_iota(jnp.int32, (rows, chan), 0) == lax.broadcasted_iota(
        jnp.int32, (rows, chan), 1
    )
    row = jnp.sum(jnp.where(diagonal, column, 0.0), axis=0, keepdims=True)
    high = row.astype(jnp.bfloat16).astype(jnp.float32)
    below = lax.broadcasted_iota(jnp.int32, (EXTRA, chan), 0)
    pair = jnp.where(below == 0, high, jnp.where(below == 1, row - high, 0.0))
    pair = pair.astype(jnp.bfloat16)
    for t in range(groups):
        out_ref[t, 0:rows] = dot(scaled, cut_ref[t]).astype(jnp.bfloat16)
        out_ref[t, rows:] = pair


def rescaled(arrived_ref, width):
    groups, rows, chan = arrived_ref.shape
    rows = rows - EXTRA
    totals = arrived_ref[0].astype(jnp.float32)
    for t in range(1, groups):
        totals = totals + arrived_ref[t].astype(jnp.float32)
    row = totals[rows : rows + 1] + totals[rows + 1 : rows + 2]
    diagonal = lax.broadcasted_iota(jnp.int32, (rows, chan), 0) == lax.broadcasted_iota(
        jnp.int32, (rows, chan), 1
    )
    squares = jnp.sum(jnp.where(diagonal, row, 0.0), axis=1, keepdims=True)
    return totals[:rows] * lax.rsqrt(squares / width + 1e-06)


def gate_kernel(flags_ref, arrived_ref, kept_ref, received_ref, out_ref, *, width):
    g = gate(flags_ref, kept_ref, received_ref, rescaled(arrived_ref, width))
    for t in range(out_ref.shape[0]):
        out_ref[t] = g


def gate_out_kernel(
    flags_ref,
    arrived_ref,
    kept_ref,
    received_ref,
    back_ref,
    out_ref,
    kept,
    received,
    buffer,
    sems,
    *,
    width,
):
    groups = out_ref.shape[0]
    size = groups // PIECES
    terms = [
        pltpu.make_async_copy(kept_ref, kept, sems.at[PIECES]),
        pltpu.make_async_copy(received_ref, received, sems.at[PIECES + 1]),
    ]
    moves = [
        pltpu.make_async_copy(
            back_ref.at[pl.ds(n * size, size)], buffer.at[pl.ds(n * size, size)], sems.at[n]
        )
        for n in range(PIECES)
    ]
    for move in terms + moves:
        move.start()
    a = rescaled(arrived_ref, width)
    for move in terms:
        move.wait()
    g = gate(flags_ref, kept, received, a)
    for t in range(groups):
        if t % size == 0:
            moves[t // size].wait()
        out_ref[t] = dot_turned(g, buffer[t]).astype(jnp.bfloat16)


def out_kernel(flags_ref, whole_ref, chunk_ref, gain_ref, gain2_ref, cut_ref, out_ref):
    groups, part, chan = cut_ref.shape
    start = pl.multiple_of(flags_ref[GROUP] * part, part)
    gain = gain_part(flags_ref, gain_ref, gain2_ref, False, start, part)
    summed = dot_turned(whole_ref[0], cut_ref[0])
    for t in range(1, groups):
        summed = summed + dot_turned(whole_ref[t], cut_ref[t])
    out_ref[...] = (chunk_ref[...].astype(jnp.float32) + gain * summed).astype(jnp.bfloat16)


def stage_kernel(source_ref, out_ref, sem):
    move = pltpu.make_async_copy(source_ref, out_ref, sem)
    move.start()
    move.wait()


def stage(array):
    return pl.pallas_call(
        stage_kernel,
        out_shape=jax.ShapeDtypeStruct(array.shape, array.dtype),
        in_specs=[pl.BlockSpec(memory_space=pl.ANY)],
        out_specs=pl.BlockSpec(memory_space=pltpu.VMEM),
        scratch_shapes=[pltpu.SemaphoreType.DMA],
        compiler_params=pltpu.CompilerParams(vmem_limit_bytes=8 << 20),
    )(array)


def pick(core, arrays, plans, like):
    def kernel(core_ref, *refs):
        sources, out_ref, sems = refs[:-2], refs[-2], refs[-1]
        for c in range(CORES):

            @pl.when(core_ref[0] == c)
            def _():
                moves = [
                    pltpu.make_async_copy(
                        sources[which].at[:, pl.ds(start, size)],
                        out_ref.at[:, pl.ds(place, size)],
                        sems.at[n],
                    )
                    for n, (which, start, place, size) in enumerate(plans[c])
                ]
                for move in moves:
                    move.start()
                for move in moves:
                    move.wait()

    return pl.pallas_call(
        kernel,
        out_shape=jax.ShapeDtypeStruct(like.shape, like.dtype),
        in_specs=[pl.BlockSpec(memory_space=pltpu.SMEM)]
        + [pl.BlockSpec(memory_space=pl.ANY)] * len(arrays),
        out_specs=pl.BlockSpec(memory_space=pltpu.VMEM),
        scratch_shapes=[pltpu.SemaphoreType.DMA((max(map(len, plans)),))],
        compiler_params=pltpu.CompilerParams(vmem_limit_bytes=8 << 20),
    )(core.reshape(1), *arrays)


def even_of(core, mine, other):
    size = mine.shape[1]
    return pick(core, [mine, other], [[(0, 0, 0, size)], [(1, 0, 0, size)]], mine)


def odd_of(core, mine, other):
    return even_of(1 - core, mine, other)


def as_row_pair(column, width):
    row = jnp.pad(column.reshape(1, -1), ((0, 0), (0, width - column.shape[0])))
    high = row.astype(jnp.bfloat16)
    low = (row - high.astype(jnp.float32)).astype(jnp.bfloat16)
    return jnp.pad(jnp.concatenate([high, low], 0), ((0, EXTRA - 2), (0, 0)))


def on_device(
    token_ids,
    block_types,
    embed_table,
    proj_weights,
    norm_gains,
    conv_filters,
    conv_caches,
    final_gain,
    unembed,
):
    f32, bf16 = jnp.float32, jnp.bfloat16
    planes = lax.axis_size("section") // CORES
    section = lax.axis_index("section")
    plane, core = section // CORES, section % CORES
    groups = lax.axis_size("tensor")
    group = lax.axis_index("tensor")
    steps, requests = token_ids.shape
    own = requests // CORES
    rows = steps * own
    vocab_local, width = embed_table.shape
    part = width // groups
    chan = proj_weights.shape[2]
    cols = unembed.shape[1]

    vocab_ids = section * vocab_local + jnp.arange(vocab_local, dtype=jnp.int32)
    table_part = lax.dynamic_slice_in_dim(embed_table, group * part, part, 1)

    def find(half):
        ids = lax.dynamic_slice_in_dim(token_ids, half * own, own, 1)
        one_hot = (ids[:, :, None] == vocab_ids).astype(bf16).reshape(rows, vocab_local)
        return jnp.dot(one_hot, table_part, preferred_element_type=f32).astype(bf16)

    on_chip = find(core) + swap_cores(find(1 - core))
    flags = jnp.stack([core, group, block_types[0]]).astype(jnp.int32)
    on_chip, flags, mine, gains, filters, history, (unembed, final_gain) = lax.optimization_barrier(
        (
            on_chip,
            flags,
            proj_weights[0].reshape(groups, part, chan),
            norm_gains,
            conv_filters[0],
            conv_caches[0].transpose(1, 0, 2),
            (unembed, final_gain),
        )
    )
    theirs, gains2 = swap_cores(mine), swap_cores(gains)

    arriving = [from_plane_behind(on_chip, distance) for distance in range(1, planes)]
    my_head = lax.dynamic_slice_in_dim(unembed, group * part, part, 0)
    head_gain = lax.dynamic_slice_in_dim(final_gain, group * part, part, 0)
    arriving, my_head, head_gain = lax.optimization_barrier((arriving, my_head, head_gain))

    work = 2 * rows * width * chan
    wide = shape((groups, rows, part))
    packed_shape = shape((groups, rows + EXTRA, chan))

    def prepare_terms(filters, history):
        kept, given = cache_terms(flags, filters, history, steps)
        return kept, swap_cores(given)

    def add_exchanged(chunk, blocks):
        return on_vmem(residual_kernel, shape((rows, part)))(
            flags, exchange(blocks), chunk, gains, gains2
        )

    def pack_partials(chunk, cut_in):
        return on_vmem(in_kernel, packed_shape, cost=work)(flags, chunk, gains, gains2, cut_in)

    def first_plane(on_chip, arriving, mine, theirs, filters, history):
        chunk, blocks = on_vmem(spread_kernel, [shape((rows, part)), wide])(
            flags, on_chip, *arriving
        )
        blocks, filters, history, mine, theirs = lax.optimization_barrier(
            (blocks, filters, history, mine, theirs)
        )
        full = exchange(blocks)
        kept, received = prepare_terms(filters, history)
        blocks = pl.pallas_call(
            native_kernel,
            out_shape=wide,
            in_specs=[pl.BlockSpec(memory_space=pltpu.SMEM)]
            + [pl.BlockSpec(memory_space=pltpu.VMEM)] * 5
            + [pl.BlockSpec(memory_space=pl.ANY)] * 2,
            out_specs=pl.BlockSpec(memory_space=pltpu.VMEM),
            scratch_shapes=[pltpu.VMEM(mine.shape, bf16)] * 2
            + [pltpu.SemaphoreType.DMA((2 * PIECES,))],
            compiler_params=pltpu.CompilerParams(vmem_limit_bytes=24 << 20),
        )(flags, full, gains, gains2, kept, received, mine, theirs)
        return add_exchanged(chunk, blocks), unset(mine), unset(mine), unset(kept), unset(kept)

    def second_plane(chunk, arriving, mine, theirs, filters, history):
        half = part // 2
        plans = [[(0, 0, 0, half)], [(1, half, 0, half)]]
        piece = exchange(pick(core, [mine, theirs], plans, mine[:, :half]))
        plans = [[(0, 0, 0, half), (1, 0, half, half)], [(1, 0, 0, half), (0, 0, half, half)]]
        cut_in = pick(core, [piece, swap_cores(piece)], plans, mine)
        return chunk, cut_in, odd_of(core, mine, theirs), *prepare_terms(filters, history)

    def last_planes(chunk, arriving, mine, theirs, filters, history):
        cut = exchange(stage(mine))
        other = swap_cores(cut)
        weights = even_of(core, cut, other), odd_of(core, cut, other)
        return chunk, *weights, *prepare_terms(filters, history)

    def half_cut_layer(chunk, packed, weight_out, kept, received):
        arrived = exchange(packed)
        blocks = pl.pallas_call(
            functools.partial(gate_out_kernel, width=width),
            out_shape=wide,
            in_specs=[pl.BlockSpec(memory_space=pltpu.SMEM)]
            + [pl.BlockSpec(memory_space=pltpu.VMEM)]
            + [pl.BlockSpec(memory_space=pl.ANY)] * 3,
            out_specs=pl.BlockSpec(memory_space=pltpu.VMEM),
            scratch_shapes=[
                pltpu.VMEM(kept.shape, f32),
                pltpu.VMEM(kept.shape, f32),
                pltpu.VMEM(weight_out.shape, bf16),
                pltpu.SemaphoreType.DMA((PIECES + 2,)),
            ],
            compiler_params=pltpu.CompilerParams(vmem_limit_bytes=24 << 20),
        )(flags, arrived, kept, received, weight_out)
        return add_exchanged(chunk, blocks)

    def cut_layer(chunk, cut_in, cut_out, kept, received):
        arrived = exchange(pack_partials(chunk, cut_in))
        kernel = on_vmem(functools.partial(gate_kernel, width=width), shape((groups, rows, chan)))
        whole = exchange(kernel(flags, arrived, kept, received))
        return on_vmem(out_kernel, shape((rows, part)), cost=work)(
            flags, whole, chunk, gains, gains2, cut_out
        )

    chunk, *held = lax.switch(
        jnp.minimum(plane, RECUT),
        [first_plane, second_plane, last_planes],
        on_chip,
        arriving,
        mine,
        theirs,
        filters,
        history,
    )
    staged = stage(lax.optimization_barrier((chunk, held[0]))[1])
    chunk = to_plane(chunk, 0, 1)
    chunk, staged, held = lax.optimization_barrier((chunk, staged, held))
    packed = pack_partials(chunk, staged)
    chunk = lax.cond(
        plane == 1, half_cut_layer, lambda c, packed, *held: c, chunk, packed, *held[1:]
    )
    staged = stage(lax.optimization_barrier((chunk, held[0]))[1])
    for layer in range(RECUT, planes):
        chunk = to_plane(chunk, layer - 1, layer)
        if layer == RECUT:
            chunk, staged = lax.optimization_barrier((chunk, staged))
        first = staged if layer == RECUT else held[0]
        chunk = cut_layer(chunk, first, *held[1:])

    last = planes - 1
    shared = jnp.where(plane == last, chunk, jnp.zeros_like(chunk))
    for target in range(last):
        shared = shared + to_plane(chunk, last, target)
    other_head = swap_cores(my_head)
    head = jnp.where(
        core == 0,
        jnp.concatenate([my_head, other_head], 1),
        jnp.concatenate([other_head, my_head], 1),
    )
    shared = shared.astype(f32)
    squares = jnp.sum(shared * shared, axis=1, keepdims=True)
    scores = jnp.dot((shared * head_gain).astype(bf16), head, preferred_element_type=f32)
    packed = jnp.concatenate([scores.astype(bf16), as_row_pair(squares, CORES * cols)], 0)
    totals = jnp.sum(exchange(copies(packed)).astype(f32), axis=0)
    square = (totals[rows] + totals[rows + 1])[:rows, None]
    logits = totals[:rows] * lax.rsqrt(square / width + 1e-06)
    kept = jnp.where(core == 0, logits[:, :cols], logits[:, cols:])
    other = swap_cores(jnp.where(core == 0, logits[:, cols:], logits[:, :cols]))
    both = jnp.where(core == 0, jnp.stack([kept, other]), jnp.stack([other, kept]))
    return both.reshape(CORES, steps, own, cols).transpose(1, 0, 2, 3).reshape(steps, requests, cols)


def solution(mesh):
    placed = (
        P(),
        P("section"),
        P("section", None),
        P("section", None, "tensor"),
        P("section", None),
        P("section", None, "tensor"),
        P("section", None, None, "tensor"),
        P(),
        P(None, "section"),
    )
    return jax.shard_map(
        on_device, mesh=mesh, in_specs=placed, out_specs=P(None, None, "section"), check_vma=False
    )
```

```python
import functools

import jax
import jax.numpy as jnp
from jax import lax
from jax.experimental import pallas as pl
from jax.experimental.pallas import tpu as pltpu
from jax.sharding import PartitionSpec as P

SHORT = 7
CORES = 2
RECUT = 2
PARTS = 4
PIECES = 4
CORE, GROUP, KIND = range(3)
EXTRA = 16


def swap_cores(block):
    devices = range(lax.axis_size("section"))
    return lax.ppermute(block, "section", [(i, i ^ 1) for i in devices])


def to_plane(block, source, target):
    route = [(CORES * source + core, CORES * target + core) for core in range(CORES)]
    return lax.ppermute(block, "section", route)


def from_plane_behind(block, distance):
    devices = lax.axis_size("section")
    route = [(i, (i + CORES * distance) % devices) for i in range(devices)]
    return lax.ppermute(block, "section", route)


def exchange(blocks):
    return lax.all_to_all(blocks, "tensor", 0, 0)


def copies(block):
    return jnp.broadcast_to(block, (lax.axis_size("tensor"),) + block.shape)


def unset(like):
    return pl.pallas_call(
        lambda out: None,
        out_shape=jax.ShapeDtypeStruct(like.shape, like.dtype),
        out_specs=pl.BlockSpec(memory_space=pl.ANY),
    )()


def on_vmem(kernel, shapes, scratch=(), cost=0):
    def call(flags, *arrays):
        return pl.pallas_call(
            kernel,
            out_shape=shapes,
            in_specs=[pl.BlockSpec(memory_space=pltpu.SMEM)]
            + [pl.BlockSpec(memory_space=pltpu.VMEM)] * len(arrays),
            out_specs=jax.tree.map(lambda _: pl.BlockSpec(memory_space=pltpu.VMEM), shapes),
            scratch_shapes=list(scratch),
            compiler_params=pltpu.CompilerParams(vmem_limit_bytes=24 << 20),
            cost_estimate=pl.CostEstimate(
                flops=cost,
                bytes_accessed=sum(a.size * a.dtype.itemsize for a in arrays),
                transcendentals=0,
            ),
        )(flags, *arrays)

    return call


def shape(dims, dtype=jnp.bfloat16):
    return jax.ShapeDtypeStruct(dims, dtype)


def terms_kernel(flags_ref, filt_ref, history_ref, kept_ref, given_ref, taps_ref):
    steps = kept_ref.shape[0]
    own = kept_ref.shape[1] - EXTRA
    taps, chan = filt_ref.shape
    length, requests, _ = history_ref.shape
    place = lax.broadcasted_iota(jnp.int32, (taps, chan), 0)
    used = (place < SHORT) | (flags_ref[KIND] == 1)
    taps_ref[0:taps] = jnp.where(used, filt_ref[...].astype(jnp.float32), 0.0)
    taps_ref[taps:] = jnp.zeros((EXTRA, chan), jnp.float32)

    def one_position(r, totals):
        row = history_ref[r].astype(jnp.float32)
        return tuple(
            total + taps_ref[pl.ds(taps - 1 + k - r, 1), :] * row for k, total in enumerate(totals)
        )

    zeros = (jnp.zeros((requests, chan), jnp.float32),) * steps
    totals = lax.fori_loop(0, length, one_position, zeros)
    first = flags_ref[CORE] == 0
    for k in range(steps):
        low, high = totals[k][:own], totals[k][own:]
        kept_ref[k, 0:own] = jnp.where(first, low, high)
        given_ref[k, 0:own] = jnp.where(first, high, low)
        lag = jnp.broadcast_to(taps_ref[k : k + 1, :], (EXTRA, chan))
        kept_ref[k, own:] = lag
        given_ref[k, own:] = lag


def cache_terms(flags, filters, history, steps):
    taps, chan = filters.shape
    length, requests, _ = history.shape
    out = shape((steps, requests // CORES + EXTRA, chan), jnp.float32)
    scratch = [pltpu.VMEM((taps + EXTRA, chan), jnp.float32)]
    cost = 2 * steps * requests * length * chan
    return on_vmem(terms_kernel, [out, out], scratch, cost)(flags, filters, history)


def gate(flags_ref, kept_ref, received_ref, a):
    steps = kept_ref.shape[0]
    own = kept_ref.shape[1] - EXTRA
    first = flags_ref[CORE] == 0

    def convolve(even, signal):
        results = []
        for k in range(steps):
            total = None
            for lag in range(k, -1, -1):
                mine, other = kept_ref[lag], received_ref[lag]
                terms = jnp.where(first, mine, other) if even else jnp.where(first, other, mine)
                if lag == k:
                    mine, other = kept_ref[k], received_ref[k]
                    base = jnp.where(first, mine, other) if even else jnp.where(first, other, mine)
                    total = base[:own]
                total = total + terms[own : own + 1] * signal[k - lag]
            results.append(total)
        return results

    a = a.astype(jnp.bfloat16).astype(jnp.float32)
    z = convolve(True, [a[k * own : (k + 1) * own] for k in range(steps)])
    z = [part.astype(jnp.bfloat16).astype(jnp.float32) for part in z]
    mixed = convolve(False, z)
    return jnp.concatenate([x * y for x, y in zip(z, mixed)], 0).astype(jnp.bfloat16)


def dot(x, y):
    return jnp.dot(x, y, preferred_element_type=jnp.float32)


def dot_turned(x, y):
    return lax.dot_general(x, y, (((1,), (1,)), ((), ())), preferred_element_type=jnp.float32)


def gain_part(flags_ref, mine_ref, other_ref, even, start, size):
    mine, other = mine_ref[:, pl.ds(start, size)], other_ref[:, pl.ds(start, size)]
    first = flags_ref[CORE] == 0
    return jnp.where(first, mine, other) if even else jnp.where(first, other, mine)


def spread_kernel(flags_ref, *refs):
    parts, (sum_ref, out_ref) = refs[:PARTS], refs[-2:]
    total = parts[0][...].astype(jnp.float32)
    for part_ref in parts[1:]:
        total = total + part_ref[...].astype(jnp.float32)
    total = total.astype(jnp.bfloat16)
    sum_ref[...] = total
    for t in range(out_ref.shape[0]):
        out_ref[t] = total


def native_kernel(
    flags_ref,
    full_ref,
    gain_ref,
    gain2_ref,
    kept_ref,
    received_ref,
    mine_ref,
    other_ref,
    out_ref,
    in_buffer,
    back_buffer,
    sems,
):
    groups, rows, part = full_ref.shape
    chan = mine_ref.shape[2]

    def moves(source_ref, buffer_ref, first):
        size = groups // PIECES
        return [
            pltpu.make_async_copy(
                source_ref.at[pl.ds(n * size, size)],
                buffer_ref.at[pl.ds(n * size, size)],
                sems.at[first + n],
            )
            for n in range(PIECES)
        ]

    for core in range(CORES):
        in_ref, back_ref = (mine_ref, other_ref) if core == 0 else (other_ref, mine_ref)

        @pl.when(flags_ref[CORE] == core)
        def _():
            ahead = moves(in_ref, in_buffer, 0)
            after = moves(back_ref, back_buffer, PIECES)
            for move in ahead:
                move.start()
            squares = jnp.zeros((rows, 1), jnp.float32)
            for t in range(groups):
                values = full_ref[t].astype(jnp.float32)
                squares = squares + jnp.sum(values * values, axis=1, keepdims=True)
            scale = lax.rsqrt(squares / (groups * part) + 1e-06)
            a = jnp.zeros((rows, chan), jnp.float32)
            for t in range(groups):
                gain = gain_part(flags_ref, gain_ref, gain2_ref, True, t * part, part)
                normed = full_ref[t].astype(jnp.float32) * scale * gain
                if t % (groups // PIECES) == 0:
                    ahead[t // (groups // PIECES)].wait()
                if t == 0:
                    for move in after:
                        move.start()
                a = a + dot(normed.astype(jnp.bfloat16), in_buffer[t])
            g = gate(flags_ref, kept_ref, received_ref, a)
            for t in range(groups):
                if t % (groups // PIECES) == 0:
                    after[t // (groups // PIECES)].wait()
                out_ref[t] = dot_turned(g, back_buffer[t]).astype(jnp.bfloat16)


def residual_kernel(flags_ref, arrived_ref, chunk_ref, gain_ref, gain2_ref, out_ref):
    groups, rows, part = arrived_ref.shape
    start = pl.multiple_of(flags_ref[GROUP] * part, part)
    gain = gain_part(flags_ref, gain_ref, gain2_ref, False, start, part)
    summed = arrived_ref[0].astype(jnp.float32)
    for t in range(1, groups):
        summed = summed + arrived_ref[t].astype(jnp.float32)
    out_ref[...] = (chunk_ref[...].astype(jnp.float32) + gain * summed).astype(jnp.bfloat16)


def in_kernel(flags_ref, chunk_ref, gain_ref, gain2_ref, cut_ref, out_ref):
    groups, part, chan = cut_ref.shape
    rows = chunk_ref.shape[0]
    start = pl.multiple_of(flags_ref[GROUP] * part, part)
    gain = gain_part(flags_ref, gain_ref, gain2_ref, True, start, part)
    values = chunk_ref[...].astype(jnp.float32)
    scaled = (values * gain).astype(jnp.bfloat16)
    column = jnp.sum(values * values, axis=1, keepdims=True)
    diagonal = lax.broadcasted_iota(jnp.int32, (rows, chan), 0) == lax.broadcasted_iota(
        jnp.int32, (rows, chan), 1
    )
    row = jnp.sum(jnp.where(diagonal, column, 0.0), axis=0, keepdims=True)
    high = row.astype(jnp.bfloat16).astype(jnp.float32)
    below = lax.broadcasted_iota(jnp.int32, (EXTRA, chan), 0)
    pair = jnp.where(below == 0, high, jnp.where(below == 1, row - high, 0.0))
    pair = pair.astype(jnp.bfloat16)
    for t in range(groups):
        out_ref[t, 0:rows] = dot(scaled, cut_ref[t]).astype(jnp.bfloat16)
        out_ref[t, rows:] = pair


def rescaled(arrived_ref, width):
    groups, rows, chan = arrived_ref.shape
    rows = rows - EXTRA
    totals = arrived_ref[0].astype(jnp.float32)
    for t in range(1, groups):
        totals = totals + arrived_ref[t].astype(jnp.float32)
    row = totals[rows : rows + 1] + totals[rows + 1 : rows + 2]
    diagonal = lax.broadcasted_iota(jnp.int32, (rows, chan), 0) == lax.broadcasted_iota(
        jnp.int32, (rows, chan), 1
    )
    squares = jnp.sum(jnp.where(diagonal, row, 0.0), axis=1, keepdims=True)
    return totals[:rows] * lax.rsqrt(squares / width + 1e-06)


def gate_kernel(flags_ref, arrived_ref, kept_ref, received_ref, out_ref, *, width):
    g = gate(flags_ref, kept_ref, received_ref, rescaled(arrived_ref, width))
    for t in range(out_ref.shape[0]):
        out_ref[t] = g


def gate_out_kernel(
    flags_ref,
    arrived_ref,
    kept_ref,
    received_ref,
    back_ref,
    out_ref,
    kept,
    received,
    buffer,
    sems,
    *,
    width,
):
    groups = out_ref.shape[0]
    size = groups // PIECES
    terms = [
        pltpu.make_async_copy(kept_ref, kept, sems.at[PIECES]),
        pltpu.make_async_copy(received_ref, received, sems.at[PIECES + 1]),
    ]
    moves = [
        pltpu.make_async_copy(
            back_ref.at[pl.ds(n * size, size)], buffer.at[pl.ds(n * size, size)], sems.at[n]
        )
        for n in range(PIECES)
    ]
    for move in terms + moves:
        move.start()
    a = rescaled(arrived_ref, width)
    for move in terms:
        move.wait()
    g = gate(flags_ref, kept, received, a)
    for t in range(groups):
        if t % size == 0:
            moves[t // size].wait()
        out_ref[t] = dot_turned(g, buffer[t]).astype(jnp.bfloat16)


def out_kernel(flags_ref, whole_ref, chunk_ref, gain_ref, gain2_ref, cut_ref, out_ref):
    groups, part, chan = cut_ref.shape
    start = pl.multiple_of(flags_ref[GROUP] * part, part)
    gain = gain_part(flags_ref, gain_ref, gain2_ref, False, start, part)
    summed = dot_turned(whole_ref[0], cut_ref[0])
    for t in range(1, groups):
        summed = summed + dot_turned(whole_ref[t], cut_ref[t])
    out_ref[...] = (chunk_ref[...].astype(jnp.float32) + gain * summed).astype(jnp.bfloat16)


def stage_kernel(source_ref, out_ref, sem):
    move = pltpu.make_async_copy(source_ref, out_ref, sem)
    move.start()
    move.wait()


def stage(array):
    return pl.pallas_call(
        stage_kernel,
        out_shape=jax.ShapeDtypeStruct(array.shape, array.dtype),
        in_specs=[pl.BlockSpec(memory_space=pl.ANY)],
        out_specs=pl.BlockSpec(memory_space=pltpu.VMEM),
        scratch_shapes=[pltpu.SemaphoreType.DMA],
        compiler_params=pltpu.CompilerParams(vmem_limit_bytes=8 << 20),
    )(array)


def pick(core, arrays, plans, like):
    def kernel(core_ref, *refs):
        sources, out_ref, sems = refs[:-2], refs[-2], refs[-1]
        for c in range(CORES):

            @pl.when(core_ref[0] == c)
            def _():
                moves = [
                    pltpu.make_async_copy(
                        sources[which].at[:, pl.ds(start, size)],
                        out_ref.at[:, pl.ds(place, size)],
                        sems.at[n],
                    )
                    for n, (which, start, place, size) in enumerate(plans[c])
                ]
                for move in moves:
                    move.start()
                for move in moves:
                    move.wait()

    return pl.pallas_call(
        kernel,
        out_shape=jax.ShapeDtypeStruct(like.shape, like.dtype),
        in_specs=[pl.BlockSpec(memory_space=pltpu.SMEM)]
        + [pl.BlockSpec(memory_space=pl.ANY)] * len(arrays),
        out_specs=pl.BlockSpec(memory_space=pltpu.VMEM),
        scratch_shapes=[pltpu.SemaphoreType.DMA((max(map(len, plans)),))],
        compiler_params=pltpu.CompilerParams(vmem_limit_bytes=8 << 20),
    )(core.reshape(1), *arrays)


def even_of(core, mine, other):
    size = mine.shape[1]
    return pick(core, [mine, other], [[(0, 0, 0, size)], [(1, 0, 0, size)]], mine)


def odd_of(core, mine, other):
    return even_of(1 - core, mine, other)


def as_row_pair(column, width):
    row = jnp.pad(column.reshape(1, -1), ((0, 0), (0, width - column.shape[0])))
    high = row.astype(jnp.bfloat16)
    low = (row - high.astype(jnp.float32)).astype(jnp.bfloat16)
    return jnp.pad(jnp.concatenate([high, low], 0), ((0, EXTRA - 2), (0, 0)))


def on_device(
    token_ids,
    block_types,
    embed_table,
    proj_weights,
    norm_gains,
    conv_filters,
    conv_caches,
    final_gain,
    unembed,
):
    f32, bf16 = jnp.float32, jnp.bfloat16
    planes = lax.axis_size("section") // CORES
    section = lax.axis_index("section")
    plane, core = section // CORES, section % CORES
    groups = lax.axis_size("tensor")
    group = lax.axis_index("tensor")
    steps, requests = token_ids.shape
    own = requests // CORES
    rows = steps * own
    vocab_local, width = embed_table.shape
    part = width // groups
    chan = proj_weights.shape[2]
    cols = unembed.shape[1]

    vocab_ids = section * vocab_local + jnp.arange(vocab_local, dtype=jnp.int32)
    table_part = lax.dynamic_slice_in_dim(embed_table, group * part, part, 1)

    def find(half):
        ids = lax.dynamic_slice_in_dim(token_ids, half * own, own, 1)
        one_hot = (ids[:, :, None] == vocab_ids).astype(bf16).reshape(rows, vocab_local)
        return jnp.dot(one_hot, table_part, preferred_element_type=f32).astype(bf16)

    on_chip = find(core) + swap_cores(find(1 - core))
    flags = jnp.stack([core, group, block_types[0]]).astype(jnp.int32)
    on_chip, flags, mine, gains, filters, history, (unembed, final_gain) = lax.optimization_barrier(
        (
            on_chip,
            flags,
            proj_weights[0].reshape(groups, part, chan),
            norm_gains,
            conv_filters[0],
            conv_caches[0].transpose(1, 0, 2),
            (unembed, final_gain),
        )
    )
    theirs, gains2 = swap_cores(mine), swap_cores(gains)

    arriving = [from_plane_behind(on_chip, distance) for distance in range(1, planes)]
    my_head = lax.dynamic_slice_in_dim(unembed, group * part, part, 0)
    head_gain = lax.dynamic_slice_in_dim(final_gain, group * part, part, 0)
    arriving, my_head, head_gain = lax.optimization_barrier((arriving, my_head, head_gain))

    work = 2 * rows * width * chan
    wide = shape((groups, rows, part))
    packed_shape = shape((groups, rows + EXTRA, chan))

    def prepare_terms(filters, history):
        kept, given = cache_terms(flags, filters, history, steps)
        return kept, swap_cores(given)

    def add_exchanged(chunk, blocks):
        return on_vmem(residual_kernel, shape((rows, part)))(
            flags, exchange(blocks), chunk, gains, gains2
        )

    def pack_partials(chunk, cut_in):
        return on_vmem(in_kernel, packed_shape, cost=work)(flags, chunk, gains, gains2, cut_in)

    def first_plane(on_chip, arriving, mine, theirs, filters, history):
        chunk, blocks = on_vmem(spread_kernel, [shape((rows, part)), wide])(
            flags, on_chip, *arriving
        )
        blocks, filters, history, mine, theirs = lax.optimization_barrier(
            (blocks, filters, history, mine, theirs)
        )
        full = exchange(blocks)
        kept, received = prepare_terms(filters, history)
        blocks = pl.pallas_call(
            native_kernel,
            out_shape=wide,
            in_specs=[pl.BlockSpec(memory_space=pltpu.SMEM)]
            + [pl.BlockSpec(memory_space=pltpu.VMEM)] * 5
            + [pl.BlockSpec(memory_space=pl.ANY)] * 2,
            out_specs=pl.BlockSpec(memory_space=pltpu.VMEM),
            scratch_shapes=[pltpu.VMEM(mine.shape, bf16)] * 2
            + [pltpu.SemaphoreType.DMA((2 * PIECES,))],
            compiler_params=pltpu.CompilerParams(vmem_limit_bytes=24 << 20),
        )(flags, full, gains, gains2, kept, received, mine, theirs)
        return add_exchanged(chunk, blocks), unset(mine), unset(mine), unset(kept), unset(kept)

    def second_plane(chunk, arriving, mine, theirs, filters, history):
        half = part // 2
        plans = [[(0, 0, 0, half)], [(1, half, 0, half)]]
        piece = exchange(pick(core, [mine, theirs], plans, mine[:, :half]))
        plans = [[(0, 0, 0, half), (1, 0, half, half)], [(1, 0, 0, half), (0, 0, half, half)]]
        cut_in = pick(core, [piece, swap_cores(piece)], plans, mine)
        return chunk, cut_in, odd_of(core, mine, theirs), *prepare_terms(filters, history)

    def last_planes(chunk, arriving, mine, theirs, filters, history):
        cut = exchange(stage(mine))
        other = swap_cores(cut)
        weights = even_of(core, cut, other), odd_of(core, cut, other)
        return chunk, *weights, *prepare_terms(filters, history)

    def half_cut_layer(chunk, packed, weight_out, kept, received):
        arrived = exchange(packed)
        blocks = pl.pallas_call(
            functools.partial(gate_out_kernel, width=width),
            out_shape=wide,
            in_specs=[pl.BlockSpec(memory_space=pltpu.SMEM)]
            + [pl.BlockSpec(memory_space=pltpu.VMEM)]
            + [pl.BlockSpec(memory_space=pl.ANY)] * 3,
            out_specs=pl.BlockSpec(memory_space=pltpu.VMEM),
            scratch_shapes=[
                pltpu.VMEM(kept.shape, f32),
                pltpu.VMEM(kept.shape, f32),
                pltpu.VMEM(weight_out.shape, bf16),
                pltpu.SemaphoreType.DMA((PIECES + 2,)),
            ],
            compiler_params=pltpu.CompilerParams(vmem_limit_bytes=24 << 20),
        )(flags, arrived, kept, received, weight_out)
        return add_exchanged(chunk, blocks)

    def cut_layer(chunk, cut_in, cut_out, kept, received):
        arrived = exchange(pack_partials(chunk, cut_in))
        kernel = on_vmem(functools.partial(gate_kernel, width=width), shape((groups, rows, chan)))
        whole = exchange(kernel(flags, arrived, kept, received))
        return on_vmem(out_kernel, shape((rows, part)), cost=work)(
            flags, whole, chunk, gains, gains2, cut_out
        )

    chunk, *held = lax.switch(
        jnp.minimum(plane, RECUT),
        [first_plane, second_plane, last_planes],
        on_chip,
        arriving,
        mine,
        theirs,
        filters,
        history,
    )
    staged = stage(lax.optimization_barrier((chunk, held[0]))[1])
    chunk = to_plane(chunk, 0, 1)
    chunk, staged, held = lax.optimization_barrier((chunk, staged, held))
    packed = pack_partials(chunk, staged)
    chunk = lax.cond(
        plane == 1, half_cut_layer, lambda c, packed, *held: c, chunk, packed, *held[1:]
    )
    staged = stage(lax.optimization_barrier((chunk, held[0]))[1])
    for layer in range(RECUT, planes):
        chunk = to_plane(chunk, layer - 1, layer)
        if layer == RECUT:
            chunk, staged = lax.optimization_barrier((chunk, staged))
        first = staged if layer == RECUT else held[0]
        chunk = cut_layer(chunk, first, *held[1:])

    last = planes - 1
    shared = jnp.where(plane == last, chunk, jnp.zeros_like(chunk))
    for target in range(last):
        shared = shared + to_plane(chunk, last, target)
    other_head = swap_cores(my_head)
    head = jnp.where(
        core == 0,
        jnp.concatenate([my_head, other_head], 1),
        jnp.concatenate([other_head, my_head], 1),
    )
    shared = shared.astype(f32)
    squares = jnp.sum(shared * shared, axis=1, keepdims=True)
    scores = jnp.dot((shared * head_gain).astype(bf16), head, preferred_element_type=f32)
    packed = jnp.concatenate([scores.astype(bf16), as_row_pair(squares, CORES * cols)], 0)
    totals = jnp.sum(exchange(copies(packed)).astype(f32), axis=0)
    square = (totals[rows] + totals[rows + 1])[:rows, None]
    logits = totals[:rows] * lax.rsqrt(square / width + 1e-06)
    kept = jnp.where(core == 0, logits[:, :cols], logits[:, cols:])
    other = swap_cores(jnp.where(core == 0, logits[:, cols:], logits[:, :cols]))
    kept, other = kept.reshape(steps, own, cols), other.reshape(steps, own, cols)
    first, second = jnp.where(core == 0, kept, other), jnp.where(core == 0, other, kept)
    return jnp.concatenate([first, second], 1)


def solution(mesh):
    placed = (
        P(),
        P("section"),
        P("section", None),
        P("section", None, "tensor"),
        P("section", None),
        P("section", None, "tensor"),
        P("section", None, None, "tensor"),
        P(),
        P(None, "section"),
    )
    return jax.shard_map(
        on_device, mesh=mesh, in_specs=placed, out_specs=P(None, None, "section"), check_vma=False
    )
```
